256 devices in a mesh: blk: 32 (over z_lo, y, core), tp: 8 (over z_hi, x).
Axes of the slice: x: 4, y: 4, z: 8 (z_hi: 2, z_lo: 4; z = z_hi * 4 + z_lo), core: 2. Of those that a mesh axis runs over, the one named last changes fastest.
Arguments:
- queries: bfloat16 [16384, 8192], P('blk', 'tp'), may hold values from -4.5 to 4.5
- leaf_kv: bfloat16 [2, 16384, 1024], P(None, 'blk', 'tp'), may hold values from -9 to 9
- root_kv: bfloat16 [2, 2048, 1024], P(None, ('blk', 'tp')), may hold values from -4.5 to 4.5
- node_kv: bfloat16 [2, 128, 256, 1024], P(None, 'blk', None, 'tp'), may hold values from -9 to 9
- node_len: int32 [128], replicated, may hold values from 64 to 256, as said below
- node_slot: int32 [128], replicated, may hold values from 0 to 127, each once
- slot_leaf: int32 [32], replicated, may hold values from 0 to 31, each once
- ancestors: int32 [32, 2], replicated, may hold values from 0 to 127, as said below
Outputs:
- attended: bfloat16 [16384, 8192], P('blk', 'tp')
The draws below stay inside these ranges and needn't reach their ends.
Inputs may be any that keep to these rules, and one draw needn't show every extreme that they name: `node_len`: every node has 64 or more tokens; some node has exactly 256. `ancestors`: column 0 holds a branch node id below 32, column 1 a twig node id of 32 or more; all leaves with one twig name the same branch; leaves per twig vary widely.
All inputs are finite; a program needn't handle non-finite values.
Results may differ from the reference program's by a relative error of at most 0.0065.
Values may be sent and summed in bfloat16 or wider, within the bound.
No kernel may reach another device: no remote copies, remote signals or barrier semaphores. Data moves between devices by JAX's collectives and lax.ppermute only.
A program may use at most 128 MiB of HBM per device.

```python
import jax
import jax.numpy as jnp
from jax import lax

HEADS = 64
KVH = 8
HD = 128
LEAF_LEN = 512
NODE_LEN = 256
DEPTH = 2
LEAVES = 32
NODES = 128
ROOT = 2048


def draw_queries(key, part):
    key = jax.random.fold_in(key, 5)
    row_count = LEAVES * LEAF_LEN
    entries = jnp.clip(jax.random.normal(key, (row_count, HEADS, HD), jnp.float32), -4.5, 4.5)
    return entries.reshape(row_count, HEADS * HD).astype(jnp.bfloat16)


def draw_root_kv(key, part):
    key = jax.random.fold_in(key, 9)
    entries = jnp.clip(2.0 * jax.random.normal(key, (2, ROOT, KVH, HD), jnp.float32), -4.5, 4.5)
    return entries.reshape(2, ROOT, KVH * HD).astype(jnp.bfloat16)


def draw_node_len(key, part):
    key = jax.random.fold_in(key, 11)
    lengths = jax.random.randint(jax.random.fold_in(key, 1), (NODES,), NODE_LEN // 4, NODE_LEN + 1)
    shuffled = jax.random.permutation(jax.random.fold_in(key, 2), NODES)
    lengths = lengths.at[shuffled[0]].set(NODE_LEN).at[shuffled[1]].set(NODE_LEN // 4)
    return lengths.astype(jnp.int32)


def draw_ancestors(key, part):
    key = jax.random.fold_in(key, 13)
    branches = max(NODES // 4, 1)
    twigs = NODES - branches
    draws = jax.random.randint(jax.random.fold_in(key, 1), (LEAVES,), 0, twigs)
    twig_ids = branches + draws * draws // twigs
    twig_ids = twig_ids.at[0].set(NODES - 1).at[1].set(branches)
    parent = jax.random.randint(jax.random.fold_in(key, 2), (NODES,), 0, branches)
    parent = parent.at[branches].set(0)
    branch_ids = parent[twig_ids]
    return jnp.stack([branch_ids, twig_ids], 1).astype(jnp.int32)


def levels(own_key, extent, cuts, least, top_value):
    level = 1.0
    for position, parts in cuts:
        steps = jax.random.uniform(jax.random.fold_in(jax.random.fold_in(own_key, 6), position), (parts,), jnp.float32, least / len(cuts), top_value / len(cuts))
        level = level * jnp.repeat(jnp.exp(steps), extent[position] // parts).reshape((-1,) + (1,) * (len(extent) - 1 - position))
    return level


def centred(key, dims, spread, bound, split=(), kind=jnp.bfloat16):
    values = spread * jax.random.normal(key, dims, jnp.float32)
    if split:
        values = values * levels(key, dims, split, -0.22, 0.18)
    return jnp.clip(values, -bound, bound).astype(kind)


def setup_inputs(seed: int = 0) -> dict:
    arg_keys = jax.random.split(jax.random.key(seed), 9)
    return {
        "queries": draw_queries(jax.random.fold_in(arg_keys[8], 71), 0),
        "leaf_kv": centred(arg_keys[1], (2, LEAVES * LEAF_LEN, KVH * HD), 2.0, 9.0, ((1, 32), (2, 8))),
        "root_kv": draw_root_kv(jax.random.fold_in(arg_keys[8], 71), 0),
        "node_kv": centred(arg_keys[3], (2, NODES, NODE_LEN, KVH * HD), 2.0, 9.0, ((1, 32), (3, 8))),
        "node_len": draw_node_len(jax.random.fold_in(arg_keys[8], 71), 0),
        "node_slot": jax.random.permutation(arg_keys[5], NODES).astype(jnp.int32),
        "slot_leaf": jax.random.permutation(arg_keys[6], LEAVES).astype(jnp.int32),
        "ancestors": draw_ancestors(jax.random.fold_in(arg_keys[8], 71), 0),
    }


masked_score = -1.0e30


def reference(queries, leaf_kv, root_kv, node_kv, node_len, node_slot, slot_leaf, ancestors):
    group = HEADS // KVH
    score_scale = HD ** -0.5
    root_keys = root_kv[0].reshape(ROOT, KVH, HD)
    root_values = root_kv[1].reshape(ROOT, KVH, HD)
    positions = jnp.arange(NODE_LEN, dtype=jnp.int32)
    causal = jnp.arange(LEAF_LEN, dtype=jnp.int32)[:, None] >= jnp.arange(LEAF_LEN, dtype=jnp.int32)[None, :]

    def one_leaf(slot_index):
        first_row = (slot_index * LEAF_LEN).astype(jnp.int32)
        query_block = lax.dynamic_slice_in_dim(queries, first_row, LEAF_LEN, 0).reshape(LEAF_LEN, KVH, group, HD)
        own_cache = lax.dynamic_slice_in_dim(leaf_kv, first_row, LEAF_LEN, 1).reshape(2, LEAF_LEN, KVH, HD)
        leaf_id = slot_leaf[slot_index]
        lineage = ancestors[leaf_id]
        stored_at = node_slot[lineage]
        lengths = node_len[lineage]
        picked = node_kv[:, stored_at].reshape(2, DEPTH * NODE_LEN, KVH, HD)
        key_rows = jnp.concatenate([root_keys, picked[0], own_cache[0]], 0)
        value_rows = jnp.concatenate([root_values, picked[1], own_cache[1]], 0)
        node_visible = (positions[None, :] < lengths[:, None]).reshape(DEPTH * NODE_LEN)
        visible = jnp.concatenate([
            jnp.ones((LEAF_LEN, ROOT), dtype=bool),
            jnp.broadcast_to(node_visible[None, :], (LEAF_LEN, DEPTH * NODE_LEN)),
            causal], 1)
        shown = visible[:, None, None, :]
        scores = jnp.einsum('qkgd,nkd->qkgn', query_block.astype(jnp.float32), key_rows.astype(jnp.float32)) * score_scale
        scores = jnp.where(shown, scores, masked_score)
        row_max = jnp.max(scores, -1, keepdims=True)
        weights = jnp.where(shown, jnp.exp(scores - row_max), 0.0)
        row_sum = jnp.sum(weights, -1)
        rounded = lax.optimization_barrier(weights.astype(jnp.bfloat16)).astype(jnp.float32)
        mixed = jnp.einsum('qkgn,nkd->qkgd', rounded, value_rows.astype(jnp.float32))
        return (mixed / row_sum[..., None]).reshape(LEAF_LEN, HEADS * HD).astype(jnp.bfloat16)

    result = lax.map(one_leaf, jnp.arange(LEAVES, dtype=jnp.int32))
    return result.reshape(LEAVES * LEAF_LEN, HEADS * HD)
```

```python
import jax
import jax.numpy as jnp
from jax import lax
from jax.experimental import pallas as pl
from jax.experimental.pallas import tpu as pltpu
from jax.sharding import PartitionSpec as P

HD = 128
HEADS_DEV = 8
LEAF_LEN = 512
NODE_LEN = 256
DEPTH = 2
ROOT = 2048
Z, Y, CORES = 4, 4, 2
CHIPS = Z * Y
PIECE = NODE_LEN // CHIPS
NODES_DEV = 4
NODE_ROWS = DEPTH * NODE_LEN

SCORE_SCALE = HD**-0.5
LOG_SCALE = SCORE_SCALE * 1.4426950408889634
MASKED = -1e30
TOTAL_MIN, TOTAL_MAX = 2.0**-60, 2.0**100

bf16, f32 = jnp.bfloat16, jnp.float32


def device_at(z, y, core):
    return (z * Y + y) * CORES + core


def shifted(dz, dy, dcore):
    return [
        (device_at(z, y, c), device_at((z + dz) % Z, (y + dy) % Y, c ^ dcore))
        for z in range(Z)
        for y in range(Y)
        for c in range(CORES)
    ]


SAME_CORE = [[device_at(z, y, c) for z in range(Z) for y in range(Y)] for c in range(CORES)]


def dot(a, b):
    return jnp.dot(a, b, preferred_element_type=f32)


def dot_t(a, b):
    return lax.dot_general(a, b, (((1,), (1,)), ((), ())), preferred_element_type=f32)


def scaled_query(q):
    scaled = q.astype(f32) * LOG_SCALE
    high = scaled.astype(bf16)
    low = (scaled - high.astype(f32)).astype(bf16)
    return jnp.concatenate([high, low], 1)


def store_keys(keys_ref, first, keys):
    count = keys.shape[0]
    turned = keys.T
    keys_ref[0:HD, first : first + count] = turned
    keys_ref[HD : 2 * HD, first : first + count] = turned


def leaf_kernel(q_ref, leaf_ref, out_ref, keys, values):
    @pl.when(pl.program_id(0) == 0)
    def _():
        store_keys(keys, 0, leaf_ref[0])
        values[:, 0:HD] = leaf_ref[1]
        values[:, HD : 2 * HD] = jnp.ones((LEAF_LEN, HD), bf16)

    half = LEAF_LEN // 2
    row = lax.broadcasted_iota(jnp.int32, (half, half), 0)
    column = lax.broadcasted_iota(jnp.int32, (half, half), 1)
    causal = row >= column
    query = scaled_query(q_ref[...])
    upper, lower = query[:half], query[half:]
    weights = jnp.exp2(jnp.where(causal, dot(upper, keys[:, :half]), MASKED)).astype(bf16)
    out_ref[0, :half, :] = dot(weights, values[:half])
    weights = jnp.exp2(dot(lower, keys[:, :half])).astype(bf16)
    own = jnp.exp2(jnp.where(causal, dot(lower, keys[:, half:]), MASKED)).astype(bf16)
    out_ref[0, half:, :] = dot(weights, values[:half]) + dot(own, values[half:])


def root_kernel(q_ref, mine_ref, other_ref, acc_ref, out_ref, keys, values):
    @pl.when(pl.program_id(0) == 0)
    def _():
        count = ROOT // CORES
        for part, ref in enumerate((mine_ref, other_ref)):
            first = part * count
            store_keys(keys, first, ref[:, 0].reshape(count, HD))
            values[first : first + count, 0:HD] = ref[:, 1].reshape(count, HD)
            values[first : first + count, HD : 2 * HD] = jnp.ones((count, HD), bf16)

    scores = dot(scaled_query(q_ref[...]), keys[...])
    out_ref[0] = acc_ref[0] + dot(jnp.exp2(scores).astype(bf16), values[...])


def select_kernel(
    blk_ref, slot_leaf_ref, ancestors_ref, node_slot_ref, mine_ref, other_ref, out_ref
):
    core = lax.rem(blk_ref[0], CORES)
    for chip in range(CHIPS):
        leaf = slot_leaf_ref[chip * CORES + core]
        for level in range(DEPTH):
            slot = node_slot_ref[ancestors_ref[leaf * DEPTH + level]]
            owner = slot // NODES_DEV
            place = lax.rem(slot, NODES_DEV)
            source = owner // CORES
            same = lax.rem(owner, CORES) == core

            @pl.when(same)
            def _():
                out_ref[chip, :, level] = mine_ref[source, :, place]

            @pl.when(jnp.logical_not(same))
            def _():
                out_ref[chip, :, level] = other_ref[source, :, place]


def node_kernel(
    blk_ref,
    slot_leaf_ref,
    ancestors_ref,
    node_len_ref,
    q_ref,
    node_ref,
    acc_ref,
    mine_ref,
    other_ref,
    leaf_ref,
    out_ref,
    keys,
    values,
    root_vmem,
    leaf_vmem,
):
    leaf = slot_leaf_ref[blk_ref[0]]
    first_len = node_len_ref[ancestors_ref[leaf * DEPTH]]
    second_len = node_len_ref[ancestors_ref[leaf * DEPTH + 1]]

    def visible(shape, dim):
        r = lax.broadcasted_iota(jnp.int32, shape, dim)
        token = (r >> 5) * PIECE + (r & (PIECE - 1))
        return token < jnp.where((r & PIECE) == 0, first_len, second_len)

    @pl.when(pl.program_id(0) == 0)
    def _():
        shown = visible((NODE_ROWS, HD), 0)
        node_keys = node_ref[:, 0].reshape(NODE_ROWS, HD).astype(f32)
        node_values = node_ref[:, 1].reshape(NODE_ROWS, HD).astype(f32)
        store_keys(keys, 0, jnp.where(shown, node_keys, 0.0).astype(bf16))
        values[:, 0:HD] = jnp.where(shown, node_values, 0.0).astype(bf16)
        values[:, HD : 2 * HD] = jnp.where(shown, 1.0, 0.0).astype(bf16)

    scores = dot(scaled_query(q_ref[...]), keys[...])
    acc = acc_ref[0] + dot(jnp.exp2(scores).astype(bf16), values[...])
    total = acc[:, HD:]
    out_ref[...] = (acc[:, :HD] / total).astype(bf16)
    inside = (total >= TOTAL_MIN) & (total <= TOTAL_MAX)
    outside = jnp.max(jnp.where(inside, 0.0, 1.0)) > 0.5

    @pl.when(outside)
    def _():
        pltpu.sync_copy(mine_ref, root_vmem.at[0])
        pltpu.sync_copy(other_ref, root_vmem.at[1])
        pltpu.sync_copy(leaf_ref, leaf_vmem)
        root_keys = root_vmem[:, :, 0].reshape(ROOT, HD)
        root_values = root_vmem[:, :, 1].reshape(ROOT, HD)
        rows = 128

        def some_rows(step, carry):
            start = pl.multiple_of(step * rows, rows)
            query = q_ref[pl.ds(start, rows), :]
            root_scores = dot_t(query, root_keys) * SCORE_SCALE
            node_scores = dot(query, keys[0:HD, :]) * SCORE_SCALE
            leaf_scores = dot_t(query, leaf_vmem[0]) * SCORE_SCALE
            node_shown = visible((rows, NODE_ROWS), 1)
            position = start + lax.broadcasted_iota(jnp.int32, (rows, LEAF_LEN), 0)
            leaf_shown = position >= lax.broadcasted_iota(jnp.int32, (rows, LEAF_LEN), 1)
            node_scores = jnp.where(node_shown, node_scores, MASKED)
            leaf_scores = jnp.where(leaf_shown, leaf_scores, MASKED)
            top = jnp.maximum(
                jnp.max(root_scores, 1, keepdims=True),
                jnp.maximum(
                    jnp.max(node_scores, 1, keepdims=True), jnp.max(leaf_scores, 1, keepdims=True)
                ),
            )
            root_weights = jnp.exp(root_scores - top)
            node_weights = jnp.where(node_shown, jnp.exp(node_scores - top), 0.0)
            leaf_weights = jnp.where(leaf_shown, jnp.exp(leaf_scores - top), 0.0)
            sums = (
                jnp.sum(root_weights, 1, keepdims=True)
                + jnp.sum(node_weights, 1, keepdims=True)
                + jnp.sum(leaf_weights, 1, keepdims=True)
            )
            mixed = (
                dot(root_weights.astype(bf16), root_values)
                + dot(node_weights.astype(bf16), values[:, 0:HD])
                + dot(leaf_weights.astype(bf16), leaf_vmem[1])
            )
            out_ref[pl.ds(start, rows), :] = (mixed / sums).astype(bf16)
            return carry

        lax.fori_loop(0, LEAF_LEN // rows, some_rows, 0)


def whole(shape):
    return pl.BlockSpec(shape, lambda h, *_: (0,) * len(shape))


q_spec = pl.BlockSpec((LEAF_LEN, HD), lambda h, *_: (0, h))
acc_spec = pl.BlockSpec((1, LEAF_LEN, 2 * HD), lambda h, *_: (h, 0, 0))
acc_shape = jax.ShapeDtypeStruct((HEADS_DEV, LEAF_LEN, 2 * HD), f32)
root_part = (CHIPS, 2, ROOT // (CHIPS * CORES), HD)


def cost(keys):
    rows = HEADS_DEV * LEAF_LEN
    return pl.CostEstimate(
        flops=rows * keys * HD * 8, bytes_accessed=2**22, transcendentals=rows * keys
    )


def attend_leaf(queries, leaf_kv):
    return pl.pallas_call(
        leaf_kernel,
        grid=(HEADS_DEV,),
        in_specs=[q_spec, whole((2, LEAF_LEN, HD))],
        out_specs=acc_spec,
        out_shape=acc_shape,
        scratch_shapes=[pltpu.VMEM((2 * HD, LEAF_LEN), bf16), pltpu.VMEM((LEAF_LEN, 2 * HD), bf16)],
        compiler_params=pltpu.CompilerParams(vmem_limit_bytes=32 * 2**20),
        cost_estimate=cost(LEAF_LEN * 3 // 4),
        name="attend_leaf",
    )(queries, leaf_kv)


def attend_root(queries, mine, other, acc):
    return pl.pallas_call(
        root_kernel,
        grid=(HEADS_DEV,),
        in_specs=[q_spec, whole(root_part), whole(root_part), acc_spec],
        out_specs=acc_spec,
        out_shape=acc_shape,
        scratch_shapes=[pltpu.VMEM((2 * HD, ROOT), bf16), pltpu.VMEM((ROOT, 2 * HD), bf16)],
        compiler_params=pltpu.CompilerParams(vmem_limit_bytes=40 * 2**20),
        cost_estimate=cost(ROOT),
        name="attend_root",
    )(queries, mine, other, acc)


def select_pieces(scalars, mine, other):
    shape = (CHIPS, 2, DEPTH, PIECE, HD)
    part = (CHIPS, 2, NODES_DEV, PIECE, HD)
    return pl.pallas_call(
        select_kernel,
        grid_spec=pltpu.PrefetchScalarGridSpec(
            num_scalar_prefetch=4,
            grid=(1,),
            in_specs=[whole(part), whole(part)],
            out_specs=whole(shape),
        ),
        out_shape=jax.ShapeDtypeStruct(shape, bf16),
        compiler_params=pltpu.CompilerParams(vmem_limit_bytes=16 * 2**20),
        name="select_pieces",
    )(*scalars, mine, other)


def attend_nodes(scalars, queries, nodes, acc, mine, other, leaf_kv):
    anywhere = pl.BlockSpec(memory_space=pl.ANY)
    return pl.pallas_call(
        node_kernel,
        grid_spec=pltpu.PrefetchScalarGridSpec(
            num_scalar_prefetch=4,
            grid=(HEADS_DEV,),
            in_specs=[
                q_spec,
                whole((CHIPS, 2, DEPTH, PIECE, HD)),
                acc_spec,
                anywhere,
                anywhere,
                anywhere,
            ],
            out_specs=q_spec,
            scratch_shapes=[
                pltpu.VMEM((2 * HD, NODE_ROWS), bf16),
                pltpu.VMEM((NODE_ROWS, 2 * HD), bf16),
                pltpu.VMEM((CORES,) + root_part, bf16),
                pltpu.VMEM((2, LEAF_LEN, HD), bf16),
            ],
        ),
        out_shape=jax.ShapeDtypeStruct((LEAF_LEN, HEADS_DEV * HD), bf16),
        compiler_params=pltpu.CompilerParams(vmem_limit_bytes=40 * 2**20),
        cost_estimate=cost(NODE_ROWS),
        name="attend_nodes",
    )(*scalars, queries, nodes, acc, mine, other, leaf_kv)


def per_device(queries, leaf_kv, root_kv, node_kv, node_len, node_slot, slot_leaf, ancestors):
    blk = lax.axis_index("blk").astype(jnp.int32).reshape(1)
    paths = ancestors.reshape(-1)

    pieces = node_kv.reshape(2, NODES_DEV, CHIPS, PIECE, HD).transpose(2, 0, 1, 3, 4)
    mine = lax.all_to_all(pieces, "blk", 0, 0, tiled=True, axis_index_groups=SAME_CORE)
    other = lax.ppermute(mine, "blk", shifted(0, 0, 1))
    chosen = select_pieces((blk, slot_leaf, paths, node_slot), mine, other)
    nodes = lax.all_to_all(chosen, "blk", 0, 0, tiled=True, axis_index_groups=SAME_CORE)

    heads = root_kv.reshape(2, -1, HEADS_DEV, HD).transpose(2, 0, 1, 3)
    heads = lax.all_to_all(heads, "tp", 0, 0, tiled=True)
    root = heads.transpose(1, 0, 2, 3).reshape(1, 2, -1, HD)
    root = jnp.concatenate([root] + [lax.ppermute(root, "blk", shifted(d, 0, 0)) for d in range(1, Z)])
    root = jnp.concatenate([root] + [lax.ppermute(root, "blk", shifted(0, d, 0)) for d in range(1, Y)])
    root_other = lax.ppermute(root, "blk", shifted(0, 0, 1))

    acc = attend_leaf(queries, leaf_kv)
    acc = attend_root(queries, root, root_other, acc)
    scalars = (blk, slot_leaf, paths, node_len)
    return attend_nodes(scalars, queries, nodes, acc, root, root_other, leaf_kv)


def solution(mesh):
    placed = (
        P("blk", "tp"),
        P(None, "blk", "tp"),
        P(None, ("blk", "tp"), None),
        P(None, "blk", None, "tp"),
        P(),
        P(),
        P(),
        P(),
    )
    return jax.shard_map(
        per_device, mesh=mesh, in_specs=placed, out_specs=P("blk", "tp"), check_vma=False
    )
```

```python
import jax
import jax.numpy as jnp
from jax import lax
from jax.experimental import pallas as pl
from jax.experimental.pallas import tpu as pltpu
from jax.sharding import PartitionSpec as P

HD = 128
HEADS_DEV = 8
LEAF_LEN = 512
NODE_LEN = 256
DEPTH = 2
ROOT = 2048
X, Y, Z, CORES = 4, 4, 4, 2
CHIPS = Z * Y
PIECE = NODE_LEN // CHIPS
NODES_DEV = 4
NODE_ROWS = DEPTH * NODE_LEN
LEAVES, NODES = 32, 128
SLOT_LEAF, ANCESTORS, NODE_SLOT, NODE_LENS, BLK = 0, 32, 96, 224, 352
SPREAD = 4
GROUP, ROOT_BLOCK = 4, 1024
SCORE_SCALE = HD**-0.5
LOG_SCALE = SCORE_SCALE * 1.4426950408889634
MASKED = -1e30
TOTAL_MIN, TOTAL_MAX = 2.0**-60, 2.0**100

bf16, f32 = jnp.bfloat16, jnp.float32


def device_at(z, y, core):
    return (z * Y + y) * CORES + core


def shifted(dz, dy, dcore):
    return [
        (device_at(z, y, c), device_at((z + dz) % Z, (y + dy) % Y, c ^ dcore))
        for z in range(Z)
        for y in range(Y)
        for c in range(CORES)
    ]


SAME_CORE = [[device_at(z, y, c) for z in range(Z) for y in range(Y)] for c in range(CORES)]


def dot(a, b):
    return jnp.dot(a, b, preferred_element_type=f32)


def dot_t(a, b):
    return lax.dot_general(a, b, (((1,), (1,)), ((), ())), preferred_element_type=f32)


def scaled_query(q):
    scaled = q.astype(f32) * LOG_SCALE
    high = scaled.astype(bf16)
    low = (scaled - high.astype(f32)).astype(bf16)
    return jnp.concatenate([high, low], 1)


def store_keys(keys_ref, first, keys):
    count = keys.shape[0]
    turned = keys.T
    keys_ref[0:HD, first : first + count] = turned
    keys_ref[HD : 2 * HD, first : first + count] = turned


def spread_kernel(node_ref, out_ref):
    for chip in range(SPREAD):
        out_ref[chip] = node_ref[:, :, chip * PIECE : (chip + 1) * PIECE]


def node_at(table_ref, blk, level):
    leaf = table_ref[SLOT_LEAF + blk]
    return table_ref[ANCESTORS + level * LEAVES + leaf]


def select_kernel(table_ref, mine_ref, other_ref, out_ref):
    core = lax.rem(table_ref[BLK], CORES)
    for chip in range(CHIPS):
        for level in range(DEPTH):
            slot = table_ref[NODE_SLOT + node_at(table_ref, chip * CORES + core, level)]
            owner = slot // NODES_DEV
            place = lax.rem(slot, NODES_DEV)
            source = owner // CORES
            out_ref[chip, :, level] = jnp.where(
                lax.rem(owner, CORES) == core,
                mine_ref[source, :, place],
                other_ref[source, :, place],
            )


def store_values(values_ref, first, rows):
    count = rows.shape[0]
    values_ref[first : first + count, 0:HD] = rows
    values_ref[first : first + count, HD : 2 * HD] = jnp.ones((count, HD), bf16)


def weigh(query, keys, values, shown=None):
    scores = dot(query, keys)
    if shown is not None:
        scores = jnp.where(shown, scores, MASKED)
    return dot(jnp.exp2(scores).astype(bf16), values)


def leaf_kernel(leaf_ref, q_ref, out_ref, keys, values):
    @pl.when(pl.program_id(0) == 0)
    def _():
        store_keys(keys, 0, leaf_ref[0])
        store_values(values, 0, leaf_ref[1])

    half = LEAF_LEN // 2
    row = lax.broadcasted_iota(jnp.int32, (half, half), 0)
    column = lax.broadcasted_iota(jnp.int32, (half, half), 1)
    causal = row >= column
    for head in range(GROUP):
        query = scaled_query(q_ref[:, head * HD : (head + 1) * HD])
        upper, lower = query[:half], query[half:]
        out_ref[head, :half] = weigh(upper, keys[:, :half], values[:half], causal)
        out_ref[head, half:] = weigh(lower, keys[:, :half], values[:half]) + weigh(
            lower, keys[:, half:], values[half:], causal
        )


def root_kernel(mine_ref, other_ref, q_ref, acc_ref, out_ref, keys, values):
    @pl.when(pl.program_id(0) == 0)
    def _():
        count = ROOT // CORES
        for part, ref in enumerate((mine_ref, other_ref)):
            store_keys(keys, part * count, ref[:, 0].reshape(count, HD))
            store_values(values, part * count, ref[:, 1].reshape(count, HD))

    for head in range(GROUP):
        query = scaled_query(q_ref[:, head * HD : (head + 1) * HD])
        acc = acc_ref[head]
        for first in range(0, ROOT, ROOT_BLOCK):
            block = slice(first, first + ROOT_BLOCK)
            acc += weigh(query, keys[:, block], values[block])
        out_ref[head] = acc


def node_kernel(
    table_ref,
    node_ref,
    mine_ref,
    other_ref,
    leaf_ref,
    q_ref,
    acc_ref,
    out_ref,
    _,
    keys,
    values,
    root_vmem,
    leaf_vmem,
):
    blk = table_ref[BLK]
    first_len = table_ref[NODE_LENS + node_at(table_ref, blk, 0)]
    second_len = table_ref[NODE_LENS + node_at(table_ref, blk, 1)]

    def visible(shape, dim):
        r = lax.broadcasted_iota(jnp.int32, shape, dim)
        token = (r >> 5) * PIECE + (r & (PIECE - 1))
        return token < jnp.where((r & PIECE) == 0, first_len, second_len)

    @pl.when(pl.program_id(0) == 0)
    def _():
        shown = visible((NODE_ROWS, HD), 0)
        node_keys = node_ref[:, 0].reshape(NODE_ROWS, HD).astype(f32)
        node_values = node_ref[:, 1].reshape(NODE_ROWS, HD).astype(f32)
        store_keys(keys, 0, jnp.where(shown, node_keys, 0.0).astype(bf16))
        values[:, 0:HD] = jnp.where(shown, node_values, 0.0).astype(bf16)
        values[:, HD : 2 * HD] = jnp.where(shown, 1.0, 0.0).astype(bf16)

    outside = jnp.zeros((LEAF_LEN, HD), f32)
    for head in range(GROUP):
        columns = slice(head * HD, (head + 1) * HD)
        acc = acc_ref[head] + weigh(scaled_query(q_ref[:, columns]), keys[...], values[...])
        total = acc[:, HD:]
        outside = jnp.where((total >= TOTAL_MIN) & (total <= TOTAL_MAX), outside, 1.0)
        out_ref[:, columns] = (acc[:, :HD] / total).astype(bf16)

    @pl.when(jnp.max(outside) > 0.5)
    def _():
        pltpu.sync_copy(mine_ref, root_vmem.at[0])
        pltpu.sync_copy(other_ref, root_vmem.at[1])
        pltpu.sync_copy(leaf_ref, leaf_vmem)
        rows = 128
        blocks = LEAF_LEN // rows

        def some_rows(step, carry):
            start = pl.multiple_of(lax.rem(step, blocks) * rows, rows)
            place = (pl.ds(start, rows), pl.ds(pl.multiple_of(step // blocks * HD, HD), HD))
            query = q_ref[place]
            root_keys = root_vmem[:, :, 0].reshape(ROOT, HD)
            root_values = root_vmem[:, :, 1].reshape(ROOT, HD)
            root_scores = dot_t(query, root_keys) * SCORE_SCALE
            node_scores = dot(query, keys[0:HD, :]) * SCORE_SCALE
            leaf_scores = dot_t(query, leaf_vmem[0]) * SCORE_SCALE
            node_shown = visible((rows, NODE_ROWS), 1)
            position = start + lax.broadcasted_iota(jnp.int32, (rows, LEAF_LEN), 0)
            leaf_shown = position >= lax.broadcasted_iota(jnp.int32, (rows, LEAF_LEN), 1)
            node_scores = jnp.where(node_shown, node_scores, MASKED)
            leaf_scores = jnp.where(leaf_shown, leaf_scores, MASKED)
            top = jnp.maximum(
                jnp.max(root_scores, 1, keepdims=True),
                jnp.maximum(
                    jnp.max(node_scores, 1, keepdims=True), jnp.max(leaf_scores, 1, keepdims=True)
                ),
            )
            root_weights = jnp.exp(root_scores - top)
            node_weights = jnp.where(node_shown, jnp.exp(node_scores - top), 0.0)
            leaf_weights = jnp.where(leaf_shown, jnp.exp(leaf_scores - top), 0.0)
            total = (
                jnp.sum(root_weights, 1, keepdims=True)
                + jnp.sum(node_weights, 1, keepdims=True)
                + jnp.sum(leaf_weights, 1, keepdims=True)
            )
            attended = (
                dot(root_weights.astype(bf16), root_values)
                + dot(node_weights.astype(bf16), values[:, 0:HD])
                + dot(leaf_weights.astype(bf16), leaf_vmem[1])
            )
            out_ref[place] = (attended / total).astype(bf16)
            return carry

        lax.fori_loop(0, GROUP * blocks, some_rows, 0)


vmem = pl.BlockSpec(memory_space=pltpu.VMEM)
smem = pl.BlockSpec(memory_space=pltpu.SMEM)
anywhere = pl.BlockSpec(memory_space=pl.ANY)
head_spec = pl.BlockSpec((LEAF_LEN, GROUP * HD), lambda step: (0, step))
acc_spec = pl.BlockSpec((GROUP, LEAF_LEN, 2 * HD), lambda step: (step, 0, 0))
root_part = (CHIPS, 2, ROOT // (CHIPS * CORES), HD)


def cost(keys):
    rows = HEADS_DEV * LEAF_LEN
    return pl.CostEstimate(
        flops=rows * keys * HD * 8, bytes_accessed=2**22, transcendentals=rows * keys
    )


def limit(mib):
    return pltpu.CompilerParams(vmem_limit_bytes=mib * 2**20)


def spread(node_kv):
    return pl.pallas_call(
        spread_kernel,
        grid=(CHIPS // SPREAD,),
        in_specs=[
            pl.BlockSpec((2, NODES_DEV, SPREAD * PIECE, HD), lambda step: (0, 0, step, 0))
        ],
        out_specs=pl.BlockSpec((SPREAD, 2, NODES_DEV, PIECE, HD), lambda step: (step, 0, 0, 0, 0)),
        out_shape=pltpu.HBM((CHIPS, 2, NODES_DEV, PIECE, HD), bf16),
        compiler_params=limit(4),
        name="spread",
    )(node_kv)


def select_pieces(table, mine, other):
    return pl.pallas_call(
        select_kernel,
        in_specs=[smem, vmem, vmem],
        out_specs=vmem,
        out_shape=jax.ShapeDtypeStruct((CHIPS, 2, DEPTH, PIECE, HD), bf16),
        compiler_params=limit(8),
        name="select_pieces",
    )(table, mine, other)


def attend_leaf(leaf_kv, queries):
    return pl.pallas_call(
        leaf_kernel,
        grid=(HEADS_DEV // GROUP,),
        in_specs=[pl.BlockSpec((2, LEAF_LEN, HD), lambda step: (0, 0, 0)), head_spec],
        out_specs=acc_spec,
        out_shape=pltpu.HBM((HEADS_DEV, LEAF_LEN, 2 * HD), f32),
        scratch_shapes=[pltpu.VMEM((2 * HD, LEAF_LEN), bf16), pltpu.VMEM((LEAF_LEN, 2 * HD), bf16)],
        compiler_params=limit(24),
        cost_estimate=cost(LEAF_LEN),
        name="attend_leaf",
    )(leaf_kv, queries)


def attend_root(mine, other, queries, acc):
    return pl.pallas_call(
        root_kernel,
        grid=(HEADS_DEV // GROUP,),
        in_specs=[vmem, vmem, head_spec, acc_spec],
        out_specs=acc_spec,
        out_shape=pltpu.HBM((HEADS_DEV, LEAF_LEN, 2 * HD), f32),
        scratch_shapes=[pltpu.VMEM((2 * HD, ROOT), bf16), pltpu.VMEM((ROOT, 2 * HD), bf16)],
        input_output_aliases={3: 0},
        compiler_params=limit(32),
        name="attend_root",
    )(mine, other, queries, acc)


def attend_nodes(table, nodes, mine, other, leaf_kv, queries, acc):
    return pl.pallas_call(
        node_kernel,
        grid=(HEADS_DEV // GROUP,),
        in_specs=[smem, vmem] + [anywhere] * 3 + [head_spec, acc_spec],
        out_specs=[head_spec, anywhere],
        out_shape=[
            jax.ShapeDtypeStruct((LEAF_LEN, HEADS_DEV * HD), bf16),
            pltpu.HBM((HEADS_DEV, LEAF_LEN, 2 * HD), f32),
        ],
        input_output_aliases={6: 1},
        scratch_shapes=[
            pltpu.VMEM((2 * HD, NODE_ROWS), bf16),
            pltpu.VMEM((NODE_ROWS, 2 * HD), bf16),
            pltpu.VMEM((CORES,) + root_part, bf16),
            pltpu.VMEM((2, LEAF_LEN, HD), bf16),
        ],
        compiler_params=limit(32),
        name="attend_nodes",
    )(table, nodes, mine, other, leaf_kv, queries, acc)[0]


def columns_of(rows, place, width):
    return lax.dynamic_slice_in_dim(rows, place * width, width, 2)


def per_device(queries, leaf_kv, root_kv, node_kv, node_len, node_slot, slot_leaf, ancestors):
    blk = lax.axis_index("blk").astype(jnp.int32).reshape(1)
    table = jnp.concatenate([slot_leaf, ancestors.T.reshape(-1), node_slot, node_len, blk])

    tp = lax.axis_index("tp").astype(jnp.int32)
    z_half, x = tp // X, tp % X
    width = X * HD
    swap = [(i, (i + X) % (2 * X)) for i in range(2 * X)]
    away = lax.ppermute(columns_of(root_kv, 1 - z_half, width), "tp", swap)
    root = jnp.concatenate([columns_of(root_kv, z_half, width), away], 1)
    parts = [columns_of(root, x, HD)]
    for d in range(1, X):
        ring = [(h * X + i, h * X + (i + d) % X) for h in range(2) for i in range(X)]
        parts.append(lax.ppermute(columns_of(root, (x + d) % X, HD), "tp", ring))
    root = jnp.concatenate(parts, 1)[None]

    root = jnp.concatenate([root] + [lax.ppermute(root, "blk", shifted(d, 0, 0)) for d in range(1, Z)])

    pieces = spread(node_kv)
    root, pieces = lax.optimization_barrier((root, pieces))
    mine = lax.all_to_all(pieces, "blk", 0, 0, tiled=True, axis_index_groups=SAME_CORE)

    acc = attend_leaf(leaf_kv, queries)
    root = jnp.concatenate([root] + [lax.ppermute(root, "blk", shifted(0, d, 0)) for d in range(1, Y)])
    root, mine, acc = lax.optimization_barrier((root, mine, acc))
    root_other = lax.ppermute(root, "blk", shifted(0, 0, 1))
    other = lax.ppermute(mine, "blk", shifted(0, 0, 1))
    chosen = select_pieces(table, mine, other)
    nodes = lax.all_to_all(chosen, "blk", 0, 0, tiled=True, axis_index_groups=SAME_CORE)

    acc = attend_root(root, root_other, queries, acc)
    return attend_nodes(table, nodes, root, root_other, leaf_kv, queries, acc)


def solution(mesh):
    placed = (
        P("blk", "tp"),
        P(None, "blk", "tp"),
        P(None, ("blk", "tp"), None),
        P(None, "blk", None, "tp"),
        P(),
        P(),
        P(),
        P(),
    )
    return jax.shard_map(
        per_device, mesh=mesh, in_specs=placed, out_specs=P("blk", "tp"), check_vma=False
    )
```

```python
import jax
import jax.numpy as jnp
from jax import lax
from jax.experimental import pallas as pl
from jax.experimental.pallas import tpu as pltpu
from jax.sharding import PartitionSpec as P

HD = 128
HEADS_DEV = 8
LEAF_LEN = 512
NODE_LEN = 256
DEPTH = 2
ROOT = 2048
X, Y, Z, CORES = 4, 4, 4, 2
CHIPS = Z * Y
PIECE = NODE_LEN // CHIPS
NODES_DEV = 4
NODE_ROWS = DEPTH * NODE_LEN
SHARED = ROOT + NODE_ROWS
KEYS = SHARED + LEAF_LEN
LEAVES = 32
SLOT_LEAF, ANCESTORS, NODE_SLOT, NODE_LENS, BLK = 0, 32, 96, 224, 352
SPREAD = 4
GROUP = 4
NODE_GROUPS = ((0, 1, 2, 3, 4, 5), (6, 7))
SCORE_SCALE = HD**-0.5
LOG_SCALE = SCORE_SCALE * 1.4426950408889634
MASKED = -1e30
TOTAL_MIN, TOTAL_MAX = 2.0**-60, 2.0**100

bf16, f32 = jnp.bfloat16, jnp.float32


def device_at(z, y, core):
    return (z * Y + y) * CORES + core


def shifted(dz, dy, dcore):
    return [
        (device_at(z, y, c), device_at((z + dz) % Z, (y + dy) % Y, c ^ dcore))
        for z in range(Z)
        for y in range(Y)
        for c in range(CORES)
    ]


SAME_CORE = [[device_at(z, y, c) for z in range(Z) for y in range(Y)] for c in range(CORES)]


def dot(a, b):
    return jnp.dot(a, b, preferred_element_type=f32)


def dot_t(a, b):
    return lax.dot_general(a, b, (((1,), (1,)), ((), ())), preferred_element_type=f32)


def scaled_query(q):
    scaled = q.astype(f32) * LOG_SCALE
    high = scaled.astype(bf16)
    low = (scaled - high.astype(f32)).astype(bf16)
    return jnp.concatenate([high, low], 1)


def store_keys(keys_ref, first, keys):
    count = keys.shape[0]
    turned = keys.T
    keys_ref[0:HD, first : first + count] = turned
    keys_ref[HD : 2 * HD, first : first + count] = turned


def spread_kernel(node_ref, out_ref):
    for chip in range(SPREAD):
        out_ref[chip] = node_ref[:, :, chip * PIECE : (chip + 1) * PIECE]


def node_at(table_ref, blk, level):
    leaf = table_ref[SLOT_LEAF + blk]
    return table_ref[ANCESTORS + level * LEAVES + leaf]


def select_kernel(table_ref, mine_ref, other_ref, out_ref):
    core = lax.rem(table_ref[BLK], CORES)
    for chip in range(CHIPS):
        for level in range(DEPTH):
            slot = table_ref[NODE_SLOT + node_at(table_ref, chip * CORES + core, level)]
            owner = slot // NODES_DEV
            place = lax.rem(slot, NODES_DEV)
            source = owner // CORES
            out_ref[chip, :, level] = jnp.where(
                lax.rem(owner, CORES) == core,
                mine_ref[source, :, place],
                other_ref[source, :, place],
            )


def store_values(values_ref, first, rows):
    count = rows.shape[0]
    values_ref[first : first + count, 0:HD] = rows
    values_ref[first : first + count, HD : 2 * HD] = jnp.ones((count, HD), bf16)


def weigh(query, keys, values, shown=None):
    scores = dot(query, keys)
    if shown is not None:
        scores = jnp.where(shown, scores, MASKED)
    return dot(jnp.exp2(scores).astype(bf16), values)


def columns_at(step, width):
    return pl.ds(pl.multiple_of(step * width, width), width)


def total_column(head):
    return head * (HD // HEADS_DEV)


def store_total(totals_ref, head, total):
    if head:
        lane = lax.broadcasted_iota(jnp.int32, (LEAF_LEN, HD), 1)
        total = jnp.where(lane >= total_column(head), total, totals_ref[...])
    totals_ref[...] = total


def store_group(copies, sums, sums_hbm, sems, head):
    if (head + 1) % GROUP == 0:
        part = slice((head + 1 - GROUP) * HD, (head + 1) * HD)
        copy = pltpu.make_async_copy(
            sums.at[:, part], sums_hbm.at[:, part], sems.at[head // GROUP]
        )
        copy.start()
        copies.append(copy)


def leaf_kernel(leaf_ref, q_ref, sums_hbm, totals_ref, keys, values, sums, sems):
    store_keys(keys, 0, leaf_ref[0])
    store_values(values, 0, leaf_ref[1])
    half = LEAF_LEN // 2
    row = lax.broadcasted_iota(jnp.int32, (half, half), 0)
    column = lax.broadcasted_iota(jnp.int32, (half, half), 1)
    causal = row >= column
    copies = []
    for head in range(HEADS_DEV):
        columns = slice(head * HD, (head + 1) * HD)
        query = scaled_query(q_ref[:, columns])
        upper, lower = query[:half], query[half:]
        acc_upper = weigh(upper, keys[:, :half], values[:half], causal)
        acc_lower = weigh(lower, keys[:, :half], values[:half]) + weigh(
            lower, keys[:, half:], values[half:], causal
        )
        sums[:half, columns] = acc_upper[:, :HD]
        sums[half:, columns] = acc_lower[:, :HD]
        store_total(totals_ref, head, jnp.concatenate([acc_upper[:, HD:], acc_lower[:, HD:]]))
        store_group(copies, sums, sums_hbm, sems, head)
    for copy in copies:
        copy.wait()


def root_kernel(mine_ref, other_ref, q_ref, sums_hbm, totals_ref, keys, values, sums, sems):
    count = ROOT // CORES
    for part, ref in enumerate((mine_ref, other_ref)):
        store_keys(keys, part * count, ref[:, 0].reshape(count, HD))
        store_values(values, part * count, ref[:, 1].reshape(count, HD))
    copies = []
    for head in range(HEADS_DEV):
        columns = slice(head * HD, (head + 1) * HD)
        acc = weigh(scaled_query(q_ref[:, columns]), keys[...], values[...])
        sums[:, columns] = acc[:, :HD]
        store_total(totals_ref, head, acc[:, HD:])
        store_group(copies, sums, sums_hbm, sems, head)
    for copy in copies:
        copy.wait()


def node_kernel(
    table_ref,
    node_ref,
    leaf_totals_ref,
    root_totals_ref,
    q_ref,
    mine_ref,
    other_ref,
    leaf_ref,
    leaf_sums_hbm,
    root_sums_hbm,
    out_ref,
    _,
    __,
    keys,
    values,
    root_vmem,
    all_keys,
    leaf_sums,
    root_sums,
    result,
    sems,
):
    arrivals = (
        pltpu.make_async_copy(leaf_sums_hbm, leaf_sums, sems.at[0]),
        pltpu.make_async_copy(root_sums_hbm, root_sums, sems.at[1]),
    )
    for arrival in arrivals:
        arrival.start()
    blk = table_ref[BLK]
    first_len = table_ref[NODE_LENS + node_at(table_ref, blk, 0)]
    second_len = table_ref[NODE_LENS + node_at(table_ref, blk, 1)]

    def visible(shape, dim):
        r = lax.broadcasted_iota(jnp.int32, shape, dim)
        token = (r >> 5) * PIECE + (r & (PIECE - 1))
        return token < jnp.where((r & PIECE) == 0, first_len, second_len)

    shown = visible((NODE_ROWS, HD), 0)
    node_keys = node_ref[:, 0].reshape(NODE_ROWS, HD).astype(f32)
    node_values = node_ref[:, 1].reshape(NODE_ROWS, HD).astype(f32)
    store_keys(keys, 0, jnp.where(shown, node_keys, 0.0).astype(bf16))
    values[:, 0:HD] = jnp.where(shown, node_values, 0.0).astype(bf16)
    values[:, HD : 2 * HD] = jnp.where(shown, 1.0, 0.0).astype(bf16)

    outside = jnp.zeros((LEAF_LEN, HD), f32)
    copies = []
    for heads in NODE_GROUPS:
        mixed = [
            weigh(scaled_query(q_ref[:, head * HD : (head + 1) * HD]), keys[...], values[...])
            for head in heads
        ]
        if not copies:
            for arrival in arrivals:
                arrival.wait()
        for head, acc in zip(heads, mixed):
            columns = slice(head * HD, (head + 1) * HD)
            place = total_column(head)
            earlier = leaf_totals_ref[...] + root_totals_ref[...]
            total = acc[:, HD:] + earlier[:, place : place + 1]
            outside = jnp.where((total >= TOTAL_MIN) & (total <= TOTAL_MAX), outside, 1.0)
            sums = acc[:, :HD] + (leaf_sums[:, columns] + root_sums[:, columns])
            result[:, columns] = (sums / total).astype(bf16)
        part = slice(heads[0] * HD, (heads[-1] + 1) * HD)
        copy = pltpu.make_async_copy(
            result.at[:, part], out_ref.at[:, part], sems.at[2 + len(copies)]
        )
        copy.start()
        copies.append(copy)
    for copy in copies:
        copy.wait()

    @pl.when(jnp.max(outside) > 0.5)
    def _():
        pltpu.sync_copy(mine_ref, root_vmem.at[0])
        pltpu.sync_copy(other_ref, root_vmem.at[1])
        pltpu.sync_copy(leaf_ref, all_keys.at[:, pl.ds(SHARED, LEAF_LEN)])
        for kind in range(2):
            all_keys[kind, 0:ROOT] = root_vmem[:, :, kind].reshape(ROOT, HD)
            all_keys[kind, ROOT:SHARED] = node_ref[:, kind].reshape(NODE_ROWS, HD)
        rows = 128
        blocks = LEAF_LEN // rows

        def some_rows(step, carry):
            start = pl.multiple_of(lax.rem(step, blocks) * rows, rows)
            place = (pl.ds(start, rows), columns_at(step // blocks, HD))
            query = q_ref[place]
            row = start + lax.broadcasted_iota(jnp.int32, (rows, NODE_ROWS), 0)
            column = lax.broadcasted_iota(jnp.int32, (rows, NODE_ROWS), 1)

            def scores_of(block):
                keys_here = all_keys[0, pl.ds(pl.multiple_of(block * NODE_ROWS, NODE_ROWS), NODE_ROWS)]
                scores = dot_t(query, keys_here) * SCORE_SCALE
                first = ROOT // NODE_ROWS
                seen = jnp.where(visible((rows, NODE_ROWS), 1), 1, 0)
                seen = jnp.where(block < first, 1, jnp.where(block == first, seen, row >= column))
                return jnp.where(seen > 0, scores, MASKED), seen > 0

            def take_top(block, top):
                return jnp.maximum(top, jnp.max(scores_of(block)[0], 1, keepdims=True))

            top = lax.fori_loop(
                0, KEYS // NODE_ROWS, take_top, jnp.full((rows, 1), MASKED, f32)
            )

            def add_block(block, carry):
                total, attended = carry
                scores, seen = scores_of(block)
                weights = jnp.where(seen, jnp.exp(scores - top), 0.0)
                here = pl.ds(pl.multiple_of(block * NODE_ROWS, NODE_ROWS), NODE_ROWS)
                total += jnp.sum(weights, 1, keepdims=True)
                return total, attended + dot(weights.astype(bf16), all_keys[1, here])

            total, attended = lax.fori_loop(
                0,
                KEYS // NODE_ROWS,
                add_block,
                (jnp.zeros((rows, 1), f32), jnp.zeros((rows, HD), f32)),
            )
            result[place] = (attended / total).astype(bf16)
            return carry

        lax.fori_loop(0, HEADS_DEV * blocks, some_rows, 0)
        pltpu.sync_copy(result, out_ref)


vmem = pl.BlockSpec(memory_space=pltpu.VMEM)
smem = pl.BlockSpec(memory_space=pltpu.SMEM)
anywhere = pl.BlockSpec(memory_space=pl.ANY)


def limit(mib):
    return pltpu.CompilerParams(vmem_limit_bytes=mib * 2**20)


def spread(node_kv):
    return pl.pallas_call(
        spread_kernel,
        grid=(CHIPS // SPREAD,),
        in_specs=[
            pl.BlockSpec((2, NODES_DEV, SPREAD * PIECE, HD), lambda step: (0, 0, step, 0))
        ],
        out_specs=pl.BlockSpec((SPREAD, 2, NODES_DEV, PIECE, HD), lambda step: (step, 0, 0, 0, 0)),
        out_shape=pltpu.HBM((CHIPS, 2, NODES_DEV, PIECE, HD), bf16),
        compiler_params=limit(4),
        name="spread",
    )(node_kv)


def select_pieces(table, mine, other):
    return pl.pallas_call(
        select_kernel,
        in_specs=[smem, vmem, vmem],
        out_specs=vmem,
        out_shape=jax.ShapeDtypeStruct((CHIPS, 2, DEPTH, PIECE, HD), bf16),
        compiler_params=limit(8),
        name="select_pieces",
    )(table, mine, other)


sums_shape = (LEAF_LEN, HEADS_DEV * HD)
totals_shape = (LEAF_LEN, HD)


sums_out = [pltpu.HBM(sums_shape, f32), jax.ShapeDtypeStruct(totals_shape, f32)]


def attend_leaf(leaf_kv, queries):
    return pl.pallas_call(
        leaf_kernel,
        in_specs=[vmem] * 2,
        out_specs=[anywhere, vmem],
        out_shape=sums_out,
        scratch_shapes=[
            pltpu.VMEM((2 * HD, LEAF_LEN), bf16),
            pltpu.VMEM((LEAF_LEN, 2 * HD), bf16),
            pltpu.VMEM(sums_shape, f32),
            pltpu.SemaphoreType.DMA((HEADS_DEV // GROUP,)),
        ],
        compiler_params=limit(16),
        name="attend_leaf",
    )(leaf_kv, queries)


def attend_root(mine, other, queries):
    return pl.pallas_call(
        root_kernel,
        in_specs=[vmem] * 3,
        out_specs=[anywhere, vmem],
        out_shape=sums_out,
        scratch_shapes=[
            pltpu.VMEM((2 * HD, ROOT), bf16),
            pltpu.VMEM((ROOT, 2 * HD), bf16),
            pltpu.VMEM(sums_shape, f32),
            pltpu.SemaphoreType.DMA((HEADS_DEV // GROUP,)),
        ],
        compiler_params=limit(32),
        name="attend_root",
    )(mine, other, queries)


def attend_nodes(table, nodes, leaf_part, root_part, queries, mine, other, leaf_kv):
    (leaf_sums, leaf_totals), (root_sums, root_totals) = leaf_part, root_part
    return pl.pallas_call(
        node_kernel,
        in_specs=[smem] + [vmem] * 4 + [anywhere] * 5,
        out_specs=[anywhere] * 3,
        out_shape=[
            jax.ShapeDtypeStruct((LEAF_LEN, HEADS_DEV * HD), bf16),
            pltpu.HBM(sums_shape, f32),
            pltpu.HBM(sums_shape, f32),
        ],
        input_output_aliases={8: 1, 9: 2},
        scratch_shapes=[
            pltpu.VMEM((2 * HD, NODE_ROWS), bf16),
            pltpu.VMEM((NODE_ROWS, 2 * HD), bf16),
            pltpu.VMEM((CORES,) + mine.shape, bf16),
            pltpu.VMEM((2, KEYS, HD), bf16),
            pltpu.VMEM(sums_shape, f32),
            pltpu.VMEM(sums_shape, f32),
            pltpu.VMEM((LEAF_LEN, HEADS_DEV * HD), bf16),
            pltpu.SemaphoreType.DMA((2 + len(NODE_GROUPS),)),
        ],
        compiler_params=limit(32),
        name="attend_nodes",
    )(
        table,
        nodes,
        leaf_totals,
        root_totals,
        queries,
        mine,
        other,
        leaf_kv,
        leaf_sums,
        root_sums,
    )[0]


def columns_of(rows, place, width):
    return lax.dynamic_slice_in_dim(rows, place * width, width, 2)


def per_device(queries, leaf_kv, root_kv, node_kv, node_len, node_slot, slot_leaf, ancestors):
    blk = lax.axis_index("blk").astype(jnp.int32).reshape(1)
    table = jnp.concatenate([slot_leaf, ancestors.T.reshape(-1), node_slot, node_len, blk])

    tp = lax.axis_index("tp").astype(jnp.int32)
    z_half, x = tp // X, tp % X
    width = X * HD
    swap = [(i, (i + X) % (2 * X)) for i in range(2 * X)]
    away = lax.ppermute(root_kv, "tp", swap)
    root = columns_of(jnp.concatenate([root_kv, away], 1), z_half, width)
    parts = [columns_of(root, x, HD)]
    for d in range(1, X):
        ring = [(h * X + i, h * X + (i + d) % X) for h in range(2) for i in range(X)]
        parts.append(lax.ppermute(columns_of(root, (x + d) % X, HD), "tp", ring))
    root = jnp.concatenate(parts, 1)[None]

    root = jnp.concatenate([root] + [lax.ppermute(root, "blk", shifted(d, 0, 0)) for d in range(1, Z)])

    pieces = spread(node_kv)
    root, pieces = lax.optimization_barrier((root, pieces))
    mine = lax.all_to_all(pieces, "blk", 0, 0, tiled=True, axis_index_groups=SAME_CORE)

    root = jnp.concatenate([root] + [lax.ppermute(root, "blk", shifted(0, d, 0)) for d in range(1, Y)])
    leaf_sums, leaf_totals = attend_leaf(leaf_kv, queries)
    root, mine, leaf_totals = lax.optimization_barrier((root, mine, leaf_totals))
    root_other = lax.ppermute(root, "blk", shifted(0, 0, 1))
    other = lax.ppermute(mine, "blk", shifted(0, 0, 1))
    chosen = select_pieces(table, mine, other)
    nodes = lax.all_to_all(chosen, "blk", 0, 0, tiled=True, axis_index_groups=SAME_CORE)

    leaf_part = leaf_sums, leaf_totals
    root_part = attend_root(root, root_other, queries)
    return attend_nodes(table, nodes, leaf_part, root_part, queries, root, root_other, leaf_kv)


def solution(mesh):
    placed = (
        P("blk", "tp"),
        P(None, "blk", "tp"),
        P(None, ("blk", "tp"), None),
        P(None, "blk", None, "tp"),
        P(),
        P(),
        P(),
        P(),
    )
    return jax.shard_map(
        per_device, mesh=mesh, in_specs=placed, out_specs=P("blk", "tp"), check_vma=False
    )
```

```python
import jax
import jax.numpy as jnp
from jax import lax
from jax.experimental import pallas as pl
from jax.experimental.pallas import tpu as pltpu
from jax.sharding import PartitionSpec as P

HD = 128
HEADS_DEV = 8
LEAF_LEN = 512
NODE_LEN = 256
DEPTH = 2
ROOT = 2048
X, Y, Z, CORES = 4, 4, 4, 2
CHIPS = Z * Y
PIECE = NODE_LEN // CHIPS
NODES_DEV = 4
NODE_ROWS = DEPTH * NODE_LEN
SHARED = ROOT + NODE_ROWS
KEYS = SHARED + LEAF_LEN
TOKENS = ROOT // (CHIPS * CORES)
NEAR = Z
LEAVES = 32
SLOT_LEAF, ANCESTORS, NODE_SLOT, NODE_LENS, BLK = 0, 32, 96, 224, 352
SPREAD = 4
GROUP = 4
NODE_GROUPS = ((0, 1, 2, 3, 4, 5), (6, 7))
SCORE_SCALE = HD**-0.5
LOG_SCALE = SCORE_SCALE * 1.4426950408889634
MASKED = -1e30
TOTAL_MIN, TOTAL_MAX = 2.0**-60, 2.0**100

bf16, f32 = jnp.bfloat16, jnp.float32


def device_at(z, y, core):
    return (z * Y + y) * CORES + core


def shifted(dz, dy, dcore):
    return [
        (device_at(z, y, c), device_at((z + dz) % Z, (y + dy) % Y, c ^ dcore))
        for z in range(Z)
        for y in range(Y)
        for c in range(CORES)
    ]


SAME_CORE = [[device_at(z, y, c) for z in range(Z) for y in range(Y)] for c in range(CORES)]


def dot(a, b):
    return jnp.dot(a, b, preferred_element_type=f32)


def dot_t(a, b):
    return lax.dot_general(a, b, (((1,), (1,)), ((), ())), preferred_element_type=f32)


def scaled_query(q):
    scaled = q.astype(f32) * LOG_SCALE
    high = scaled.astype(bf16)
    low = (scaled - high.astype(f32)).astype(bf16)
    return jnp.concatenate([high, low], 1)


def store_keys(keys_ref, first, keys):
    count = keys.shape[0]
    turned = keys.T
    keys_ref[0:HD, first : first + count] = turned
    keys_ref[HD : 2 * HD, first : first + count] = turned


def spread_kernel(node_ref, out_ref):
    for chip in range(SPREAD):
        out_ref[chip] = node_ref[:, :, chip * PIECE : (chip + 1) * PIECE]


def node_at(table_ref, blk, level):
    leaf = table_ref[SLOT_LEAF + blk]
    return table_ref[ANCESTORS + level * LEAVES + leaf]


def select_kernel(table_ref, mine_ref, other_ref, out_ref):
    core = lax.rem(table_ref[BLK], CORES)
    for chip in range(CHIPS):
        for level in range(DEPTH):
            slot = table_ref[NODE_SLOT + node_at(table_ref, chip * CORES + core, level)]
            owner = slot // NODES_DEV
            place = lax.rem(slot, NODES_DEV)
            source = owner // CORES
            out_ref[chip, :, level] = jnp.where(
                lax.rem(owner, CORES) == core,
                mine_ref[source, :, place],
                other_ref[source, :, place],
            )


def store_values(values_ref, first, rows):
    count = rows.shape[0]
    values_ref[first : first + count, 0:HD] = rows
    values_ref[first : first + count, HD : 2 * HD] = jnp.ones((count, HD), bf16)


def weigh(query, keys, values, shown=None):
    scores = dot(query, keys)
    if shown is not None:
        scores = jnp.where(shown, scores, MASKED)
    return dot(jnp.exp2(scores).astype(bf16), values)


def columns_at(step, width):
    return pl.ds(pl.multiple_of(step * width, width), width)


def total_column(head):
    return head * (HD // HEADS_DEV)


def store_total(totals_ref, head, total):
    if head:
        lane = lax.broadcasted_iota(jnp.int32, (LEAF_LEN, HD), 1)
        total = jnp.where(lane >= total_column(head), total, totals_ref[...])
    totals_ref[...] = total


def store_group(copies, sums, sums_hbm, sems, head):
    if (head + 1) % GROUP == 0:
        part = slice((head + 1 - GROUP) * HD, (head + 1) * HD)
        copy = pltpu.make_async_copy(
            sums.at[:, part], sums_hbm.at[:, part], sems.at[head // GROUP]
        )
        copy.start()
        copies.append(copy)


def store_root(keys, values, first, parts):
    count = parts.shape[0] * parts.shape[2]
    store_keys(keys, first, parts[:, 0].reshape(count, HD))
    store_values(values, first, parts[:, 1].reshape(count, HD))


def near_kernel(
    table_ref,
    root_ref,
    leaf_ref,
    q_ref,
    sums_hbm,
    totals_ref,
    down_ref,
    along_ref,
    keys,
    values,
    sums,
    sems,
):
    blk = table_ref[BLK]
    first_len = table_ref[NODE_LENS + node_at(table_ref, blk, 0)]
    second_len = table_ref[NODE_LENS + node_at(table_ref, blk, 1)]
    for ref, dim in ((down_ref, 0), (along_ref, 1)):
        r = lax.broadcasted_iota(jnp.int32, ref.shape, dim)
        token = (r >> 5) * PIECE + (r & (PIECE - 1))
        length = jnp.where((r & PIECE) == 0, first_len, second_len)
        ref[...] = jnp.where(token < length, 1.0, 0.0)
    near = NEAR * TOKENS
    store_root(keys, values, 0, root_ref)
    store_keys(keys, near, leaf_ref[0])
    store_values(values, near, leaf_ref[1])
    half = LEAF_LEN // 2
    middle, last = near + half, near + LEAF_LEN
    row = lax.broadcasted_iota(jnp.int32, (half, half), 0)
    column = lax.broadcasted_iota(jnp.int32, (half, half), 1)
    causal = row >= column
    copies = []
    for head in range(HEADS_DEV):
        columns = slice(head * HD, (head + 1) * HD)
        query = scaled_query(q_ref[:, columns])
        upper, lower = query[:half], query[half:]
        acc_upper = weigh(upper, keys[:, :near], values[:near]) + weigh(
            upper, keys[:, near:middle], values[near:middle], causal
        )
        acc_lower = weigh(lower, keys[:, :middle], values[:middle]) + weigh(
            lower, keys[:, middle:last], values[middle:last], causal
        )
        sums[:half, columns] = acc_upper[:, :HD]
        sums[half:, columns] = acc_lower[:, :HD]
        store_total(totals_ref, head, jnp.concatenate([acc_upper[:, HD:], acc_lower[:, HD:]]))
        store_group(copies, sums, sums_hbm, sems, head)
    for copy in copies:
        copy.wait()


def far_kernel(mine_ref, other_ref, q_ref, sums_hbm, totals_ref, keys, values, sums, sems):
    store_root(keys, values, 0, mine_ref[NEAR:])
    store_root(keys, values, (CHIPS - NEAR) * TOKENS, other_ref)
    copies = []
    for head in range(HEADS_DEV):
        columns = slice(head * HD, (head + 1) * HD)
        acc = weigh(scaled_query(q_ref[:, columns]), keys[...], values[...])
        sums[:, columns] = acc[:, :HD]
        store_total(totals_ref, head, acc[:, HD:])
        store_group(copies, sums, sums_hbm, sems, head)
    for copy in copies:
        copy.wait()


def node_kernel(
    node_ref,
    down_ref,
    along_ref,
    near_totals_ref,
    far_totals_ref,
    q_ref,
    mine_ref,
    other_ref,
    leaf_ref,
    near_sums_hbm,
    far_sums_hbm,
    out_ref,
    _,
    __,
    keys,
    values,
    root_vmem,
    all_keys,
    near_sums,
    far_sums,
    result,
    sems,
):
    arrivals = (
        pltpu.make_async_copy(near_sums_hbm, near_sums, sems.at[0]),
        pltpu.make_async_copy(far_sums_hbm, far_sums, sems.at[1]),
    )
    for arrival in arrivals:
        arrival.start()
    shown = down_ref[...] > 0.5
    node_keys = node_ref[:, 0].reshape(NODE_ROWS, HD).astype(f32)
    node_values = node_ref[:, 1].reshape(NODE_ROWS, HD).astype(f32)
    store_keys(keys, 0, jnp.where(shown, node_keys, 0.0).astype(bf16))
    values[:, 0:HD] = jnp.where(shown, node_values, 0.0).astype(bf16)
    values[:, HD : 2 * HD] = down_ref[...].astype(bf16)

    outside = jnp.zeros((LEAF_LEN, HD), f32)
    copies = []
    for heads in NODE_GROUPS:
        mixed = [
            weigh(scaled_query(q_ref[:, head * HD : (head + 1) * HD]), keys[...], values[...])
            for head in heads
        ]
        if not copies:
            for arrival in arrivals:
                arrival.wait()
        for head, acc in zip(heads, mixed):
            columns = slice(head * HD, (head + 1) * HD)
            place = total_column(head)
            earlier = near_totals_ref[...] + far_totals_ref[...]
            total = acc[:, HD:] + earlier[:, place : place + 1]
            outside = jnp.where((total >= TOTAL_MIN) & (total <= TOTAL_MAX), outside, 1.0)
            sums = acc[:, :HD] + (near_sums[:, columns] + far_sums[:, columns])
            result[:, columns] = (sums / total).astype(bf16)
        part = slice(heads[0] * HD, (heads[-1] + 1) * HD)
        copy = pltpu.make_async_copy(
            result.at[:, part], out_ref.at[:, part], sems.at[2 + len(copies)]
        )
        copy.start()
        copies.append(copy)
    for copy in copies:
        copy.wait()

    @pl.when(jnp.max(outside) > 0.5)
    def _():
        pltpu.sync_copy(mine_ref, root_vmem.at[0])
        pltpu.sync_copy(other_ref, root_vmem.at[1])
        pltpu.sync_copy(leaf_ref, all_keys.at[:, pl.ds(SHARED, LEAF_LEN)])
        for kind in range(2):
            all_keys[kind, 0:ROOT] = root_vmem[:, :, kind].reshape(ROOT, HD)
            all_keys[kind, ROOT:SHARED] = node_ref[:, kind].reshape(NODE_ROWS, HD)
        rows = 128
        blocks = LEAF_LEN // rows

        def some_rows(step, carry):
            start = pl.multiple_of(lax.rem(step, blocks) * rows, rows)
            place = (pl.ds(start, rows), columns_at(step // blocks, HD))
            query = q_ref[place]
            row = start + lax.broadcasted_iota(jnp.int32, (rows, NODE_ROWS), 0)
            column = lax.broadcasted_iota(jnp.int32, (rows, NODE_ROWS), 1)

            def scores_of(block):
                keys_here = all_keys[0, pl.ds(pl.multiple_of(block * NODE_ROWS, NODE_ROWS), NODE_ROWS)]
                scores = dot_t(query, keys_here) * SCORE_SCALE
                first = ROOT // NODE_ROWS
                seen = jnp.where(jnp.broadcast_to(along_ref[0:1], row.shape) > 0.5, 1, 0)
                seen = jnp.where(block < first, 1, jnp.where(block == first, seen, row >= column))
                return jnp.where(seen > 0, scores, MASKED), seen > 0

            def take_top(block, top):
                return jnp.maximum(top, jnp.max(scores_of(block)[0], 1, keepdims=True))

            top = lax.fori_loop(
                0, KEYS // NODE_ROWS, take_top, jnp.full((rows, 1), MASKED, f32)
            )

            def add_block(block, carry):
                total, attended = carry
                scores, seen = scores_of(block)
                weights = jnp.where(seen, jnp.exp(scores - top), 0.0)
                here = pl.ds(pl.multiple_of(block * NODE_ROWS, NODE_ROWS), NODE_ROWS)
                total += jnp.sum(weights, 1, keepdims=True)
                return total, attended + dot(weights.astype(bf16), all_keys[1, here])

            total, attended = lax.fori_loop(
                0,
                KEYS // NODE_ROWS,
                add_block,
                (jnp.zeros((rows, 1), f32), jnp.zeros((rows, HD), f32)),
            )
            result[place] = (attended / total).astype(bf16)
            return carry

        lax.fori_loop(0, HEADS_DEV * blocks, some_rows, 0)
        pltpu.sync_copy(result, out_ref)


vmem = pl.BlockSpec(memory_space=pltpu.VMEM)
smem = pl.BlockSpec(memory_space=pltpu.SMEM)
anywhere = pl.BlockSpec(memory_space=pl.ANY)


def limit(mib):
    return pltpu.CompilerParams(vmem_limit_bytes=mib * 2**20)


def spread(node_kv):
    return pl.pallas_call(
        spread_kernel,
        grid=(CHIPS // SPREAD,),
        in_specs=[
            pl.BlockSpec((2, NODES_DEV, SPREAD * PIECE, HD), lambda step: (0, 0, step, 0))
        ],
        out_specs=pl.BlockSpec((SPREAD, 2, NODES_DEV, PIECE, HD), lambda step: (step, 0, 0, 0, 0)),
        out_shape=pltpu.HBM((CHIPS, 2, NODES_DEV, PIECE, HD), bf16),
        compiler_params=limit(4),
        name="spread",
    )(node_kv)


def select_pieces(table, mine, other):
    return pl.pallas_call(
        select_kernel,
        in_specs=[smem, vmem, vmem],
        out_specs=vmem,
        out_shape=jax.ShapeDtypeStruct((CHIPS, 2, DEPTH, PIECE, HD), bf16),
        compiler_params=limit(8),
        name="select_pieces",
    )(table, mine, other)


sums_shape = (LEAF_LEN, HEADS_DEV * HD)
totals_shape = (LEAF_LEN, HD)


sums_out = [pltpu.HBM(sums_shape, f32), jax.ShapeDtypeStruct(totals_shape, f32)]


def attend_near(table, root, leaf_kv, queries):
    count = NEAR * TOKENS + LEAF_LEN
    return pl.pallas_call(
        near_kernel,
        in_specs=[smem] + [vmem] * 3,
        out_specs=[anywhere, vmem, vmem, vmem],
        out_shape=sums_out
        + [
            jax.ShapeDtypeStruct((NODE_ROWS, HD), f32),
            jax.ShapeDtypeStruct((8, NODE_ROWS), f32),
        ],
        scratch_shapes=[
            pltpu.VMEM((2 * HD, count), bf16),
            pltpu.VMEM((count, 2 * HD), bf16),
            pltpu.VMEM(sums_shape, f32),
            pltpu.SemaphoreType.DMA((HEADS_DEV // GROUP,)),
        ],
        compiler_params=limit(24),
        name="attend_near",
    )(table, root, leaf_kv, queries)


def attend_far(mine, other, queries):
    count = ROOT - NEAR * TOKENS
    return pl.pallas_call(
        far_kernel,
        in_specs=[vmem] * 3,
        out_specs=[anywhere, vmem],
        out_shape=sums_out,
        scratch_shapes=[
            pltpu.VMEM((2 * HD, count), bf16),
            pltpu.VMEM((count, 2 * HD), bf16),
            pltpu.VMEM(sums_shape, f32),
            pltpu.SemaphoreType.DMA((HEADS_DEV // GROUP,)),
        ],
        compiler_params=limit(32),
        name="attend_far",
    )(mine, other, queries)


def attend_nodes(nodes, masks, near_part, far_part, queries, mine, other, leaf_kv):
    (near_sums, near_totals), (far_sums, far_totals) = near_part, far_part
    return pl.pallas_call(
        node_kernel,
        in_specs=[vmem] * 6 + [anywhere] * 5,
        out_specs=[anywhere] * 3,
        out_shape=[
            jax.ShapeDtypeStruct((LEAF_LEN, HEADS_DEV * HD), bf16),
            pltpu.HBM(sums_shape, f32),
            pltpu.HBM(sums_shape, f32),
        ],
        input_output_aliases={9: 1, 10: 2},
        scratch_shapes=[
            pltpu.VMEM((2 * HD, NODE_ROWS), bf16),
            pltpu.VMEM((NODE_ROWS, 2 * HD), bf16),
            pltpu.VMEM((CORES,) + mine.shape, bf16),
            pltpu.VMEM((2, KEYS, HD), bf16),
            pltpu.VMEM(sums_shape, f32),
            pltpu.VMEM(sums_shape, f32),
            pltpu.VMEM((LEAF_LEN, HEADS_DEV * HD), bf16),
            pltpu.SemaphoreType.DMA((2 + len(NODE_GROUPS),)),
        ],
        compiler_params=limit(32),
        name="attend_nodes",
    )(
        nodes,
        *masks,
        near_totals,
        far_totals,
        queries,
        mine,
        other,
        leaf_kv,
        near_sums,
        far_sums,
    )[0]


def columns_of(rows, place, width):
    return lax.dynamic_slice_in_dim(rows, place * width, width, 2)


def per_device(queries, leaf_kv, root_kv, node_kv, node_len, node_slot, slot_leaf, ancestors):
    blk = lax.axis_index("blk").astype(jnp.int32).reshape(1)
    table = jnp.concatenate([slot_leaf, ancestors.T.reshape(-1), node_slot, node_len, blk])

    tp = lax.axis_index("tp").astype(jnp.int32)
    z_half, x = tp // X, tp % X
    width = X * HD
    swap = [(i, (i + X) % (2 * X)) for i in range(2 * X)]
    away = lax.ppermute(root_kv, "tp", swap)
    root = columns_of(jnp.concatenate([root_kv, away], 1), z_half, width)
    parts = [columns_of(root, x, HD)]
    for d in range(1, X):
        ring = [(h * X + i, h * X + (i + d) % X) for h in range(2) for i in range(X)]
        parts.append(lax.ppermute(columns_of(root, (x + d) % X, HD), "tp", ring))
    root = jnp.concatenate(parts, 1)[None]

    root = jnp.concatenate([root] + [lax.ppermute(root, "blk", shifted(d, 0, 0)) for d in range(1, Z)])

    pieces = spread(node_kv)
    root, pieces = lax.optimization_barrier((root, pieces))
    mine = lax.all_to_all(pieces, "blk", 0, 0, tiled=True, axis_index_groups=SAME_CORE)

    near_sums, near_totals, *masks = attend_near(table, root, leaf_kv, queries)
    root = jnp.concatenate([root] + [lax.ppermute(root, "blk", shifted(0, d, 0)) for d in range(1, Y)])
    root, mine, near_totals = lax.optimization_barrier((root, mine, near_totals))
    root_other = lax.ppermute(root, "blk", shifted(0, 0, 1))
    other = lax.ppermute(mine, "blk", shifted(0, 0, 1))
    chosen = select_pieces(table, mine, other)
    nodes = lax.all_to_all(chosen, "blk", 0, 0, tiled=True, axis_index_groups=SAME_CORE)

    near_part = near_sums, near_totals
    far_part = attend_far(root, root_other, queries)
    return attend_nodes(nodes, masks, near_part, far_part, queries, root, root_other, leaf_kv)


def solution(mesh):
    placed = (
        P("blk", "tp"),
        P(None, "blk", "tp"),
        P(None, ("blk", "tp"), None),
        P(None, "blk", None, "tp"),
        P(),
        P(),
        P(),
        P(),
    )
    return jax.shard_map(
        per_device, mesh=mesh, in_specs=placed, out_specs=P("blk", "tp"), check_vma=False
    )
```

```python
import jax
import jax.numpy as jnp
from jax import lax
from jax.experimental import pallas as pl
from jax.experimental.pallas import tpu as pltpu
from jax.sharding import PartitionSpec as P

HD = 128
HEADS_DEV = 8
LEAF_LEN = 512
NODE_LEN = 256
DEPTH = 2
ROOT = 2048
X, Y, Z, CORES = 4, 4, 4, 2
CHIPS = Z * Y
PIECE = NODE_LEN // CHIPS
NODES_DEV = 4
NODE_ROWS = DEPTH * NODE_LEN
SHARED = ROOT + NODE_ROWS
KEYS = SHARED + LEAF_LEN
TOKENS = ROOT // (CHIPS * CORES)
NEAR = Z
LEAVES = 32
SLOT_LEAF, ANCESTORS, NODE_SLOT, NODE_LENS, BLK = 0, 32, 96, 224, 352
SPREAD = 4
GROUP = 4
NODE_GROUPS = ((0, 1, 2, 3, 4, 5), (6, 7))
EARLY_HEADS = 5
FAR_EARLY_HEADS = 2
SCORE_SCALE = HD**-0.5
LOG_SCALE = SCORE_SCALE * 1.4426950408889634
MASKED = -1e30
TOTAL_MIN, TOTAL_MAX = 2.0**-60, 2.0**100

bf16, f32 = jnp.bfloat16, jnp.float32


def device_at(z, y, core):
    return (z * Y + y) * CORES + core


def shifted(dz, dy, dcore):
    return [
        (device_at(z, y, c), device_at((z + dz) % Z, (y + dy) % Y, c ^ dcore))
        for z in range(Z)
        for y in range(Y)
        for c in range(CORES)
    ]


SAME_CORE = [[device_at(z, y, c) for z in range(Z) for y in range(Y)] for c in range(CORES)]


def dot(a, b):
    return jnp.dot(a, b, preferred_element_type=f32)


def dot_t(a, b):
    return lax.dot_general(a, b, (((1,), (1,)), ((), ())), preferred_element_type=f32)


def scaled_query(q):
    scaled = q.astype(f32) * LOG_SCALE
    high = scaled.astype(bf16)
    low = (scaled - high.astype(f32)).astype(bf16)
    return jnp.concatenate([high, low], 1)


def store_keys(keys_ref, first, keys):
    count = keys.shape[0]
    turned = keys.T
    keys_ref[0:HD, first : first + count] = turned
    keys_ref[HD : 2 * HD, first : first + count] = turned


def spread_kernel(node_ref, out_ref):
    for chip in range(SPREAD):
        out_ref[chip] = node_ref[:, :, chip * PIECE : (chip + 1) * PIECE]


def node_at(table_ref, blk, level):
    leaf = table_ref[SLOT_LEAF + blk]
    return table_ref[ANCESTORS + level * LEAVES + leaf]


def select_kernel(table_ref, mine_ref, other_ref, out_ref):
    core = lax.rem(table_ref[BLK], CORES)
    for chip in range(CHIPS):
        for level in range(DEPTH):
            slot = table_ref[NODE_SLOT + node_at(table_ref, chip * CORES + core, level)]
            owner = slot // NODES_DEV
            place = lax.rem(slot, NODES_DEV)
            source = owner // CORES
            out_ref[chip, :, level] = jnp.where(
                lax.rem(owner, CORES) == core,
                mine_ref[source, :, place],
                other_ref[source, :, place],
            )


def store_values(values_ref, first, rows):
    count = rows.shape[0]
    values_ref[first : first + count, 0:HD] = rows
    values_ref[first : first + count, HD : 2 * HD] = jnp.ones((count, HD), bf16)


def weigh(query, keys, values, shown=None):
    scores = dot(query, keys)
    if shown is not None:
        scores = jnp.where(shown, scores, MASKED)
    return dot(jnp.exp2(scores).astype(bf16), values)


def columns_at(step, width):
    return pl.ds(pl.multiple_of(step * width, width), width)


def total_column(head):
    return head * (HD // HEADS_DEV)


def store_total(totals_ref, head, total):
    if head:
        lane = lax.broadcasted_iota(jnp.int32, (LEAF_LEN, HD), 1)
        total = jnp.where(lane >= total_column(head), total, totals_ref[...])
    totals_ref[...] = total


def store_group(copies, sums, sums_hbm, sems, head):
    if (head + 1) % GROUP == 0:
        part = slice((head + 1 - GROUP) * HD, (head + 1) * HD)
        copy = pltpu.make_async_copy(
            sums.at[:, part], sums_hbm.at[:, part], sems.at[head // GROUP]
        )
        copy.start()
        copies.append(copy)


def store_root(keys, values, first, parts):
    count = parts.shape[0] * parts.shape[2]
    store_keys(keys, first, parts[:, 0].reshape(count, HD))
    store_values(values, first, parts[:, 1].reshape(count, HD))


def near_kernel(
    table_ref,
    root_ref,
    leaf_ref,
    q_ref,
    sums_hbm,
    totals_ref,
    down_ref,
    along_ref,
    keys,
    values,
    sums,
    sems,
):
    blk = table_ref[BLK]
    first_len = table_ref[NODE_LENS + node_at(table_ref, blk, 0)]
    second_len = table_ref[NODE_LENS + node_at(table_ref, blk, 1)]
    for ref, dim in ((down_ref, 0), (along_ref, 1)):
        r = lax.broadcasted_iota(jnp.int32, ref.shape, dim)
        token = (r >> 5) * PIECE + (r & (PIECE - 1))
        length = jnp.where((r & PIECE) == 0, first_len, second_len)
        ref[...] = jnp.where(token < length, 1.0, 0.0)
    near = NEAR * TOKENS
    store_root(keys, values, 0, root_ref)
    store_keys(keys, near, leaf_ref[0])
    store_values(values, near, leaf_ref[1])
    half = LEAF_LEN // 2
    middle, last = near + half, near + LEAF_LEN
    row = lax.broadcasted_iota(jnp.int32, (half, half), 0)
    column = lax.broadcasted_iota(jnp.int32, (half, half), 1)
    causal = row >= column
    copies = []
    for head in range(HEADS_DEV):
        columns = slice(head * HD, (head + 1) * HD)
        query = scaled_query(q_ref[:, columns])
        upper, lower = query[:half], query[half:]
        acc_upper = weigh(upper, keys[:, :near], values[:near]) + weigh(
            upper, keys[:, near:middle], values[near:middle], causal
        )
        acc_lower = weigh(lower, keys[:, :middle], values[:middle]) + weigh(
            lower, keys[:, middle:last], values[middle:last], causal
        )
        sums[:half, columns] = acc_upper[:, :HD]
        sums[half:, columns] = acc_lower[:, :HD]
        store_total(totals_ref, head, jnp.concatenate([acc_upper[:, HD:], acc_lower[:, HD:]]))
        store_group(copies, sums, sums_hbm, sems, head)
    for copy in copies:
        copy.wait()


def far_kernel(
    mine_ref,
    other_ref,
    q_ref,
    near_totals_ref,
    near_sums_hbm,
    sums_hbm,
    totals_ref,
    keys,
    values,
    sums,
    sems,
):
    arrival = pltpu.make_async_copy(near_sums_hbm, sums, sems.at[HEADS_DEV // GROUP])
    arrival.start()
    store_root(keys, values, 0, mine_ref[NEAR:])
    store_root(keys, values, (CHIPS - NEAR) * TOKENS, other_ref)
    copies = []
    held = []
    for head in range(HEADS_DEV):
        columns = slice(head * HD, (head + 1) * HD)
        held.append((head, weigh(scaled_query(q_ref[:, columns]), keys[...], values[...])))
        if head + 1 < FAR_EARLY_HEADS:
            continue
        if head + 1 == FAR_EARLY_HEADS:
            arrival.wait()
        for place, acc in held:
            columns = slice(place * HD, (place + 1) * HD)
            sums[:, columns] += acc[:, :HD]
            store_total(totals_ref, place, acc[:, HD:])
            store_group(copies, sums, sums_hbm, sems, place)
        held = []
    totals_ref[...] += near_totals_ref[...]
    for copy in copies:
        copy.wait()


def node_kernel(
    node_ref,
    down_ref,
    along_ref,
    totals_ref,
    q_ref,
    mine_ref,
    other_ref,
    leaf_ref,
    sums_hbm,
    out_ref,
    _,
    keys,
    values,
    root_vmem,
    all_keys,
    earlier_sums,
    result,
    sems,
):
    arrival = pltpu.make_async_copy(sums_hbm, earlier_sums, sems.at[0])
    arrival.start()
    shown = down_ref[...] > 0.5
    node_keys = node_ref[:, 0].reshape(NODE_ROWS, HD).astype(f32)
    node_values = node_ref[:, 1].reshape(NODE_ROWS, HD).astype(f32)
    store_keys(keys, 0, jnp.where(shown, node_keys, 0.0).astype(bf16))
    values[:, 0:HD] = jnp.where(shown, node_values, 0.0).astype(bf16)
    values[:, HD : 2 * HD] = down_ref[...].astype(bf16)

    outside = jnp.zeros((LEAF_LEN, HD), f32)
    copies = []
    held = []
    for heads in NODE_GROUPS:
        for head in heads:
            columns = slice(head * HD, (head + 1) * HD)
            held.append((head, weigh(scaled_query(q_ref[:, columns]), keys[...], values[...])))
            if head + 1 < EARLY_HEADS:
                continue
            if head + 1 == EARLY_HEADS:
                arrival.wait()
            for place, acc in held:
                columns = slice(place * HD, (place + 1) * HD)
                first = total_column(place)
                total = acc[:, HD:] + totals_ref[:, first : first + 1]
                outside = jnp.where((total >= TOTAL_MIN) & (total <= TOTAL_MAX), outside, 1.0)
                sums = acc[:, :HD] + earlier_sums[:, columns]
                result[:, columns] = (sums / total).astype(bf16)
            held = []
        part = slice(heads[0] * HD, (heads[-1] + 1) * HD)
        copy = pltpu.make_async_copy(
            result.at[:, part], out_ref.at[:, part], sems.at[1 + len(copies)]
        )
        copy.start()
        copies.append(copy)
    for copy in copies:
        copy.wait()

    @pl.when(jnp.max(outside) > 0.5)
    def _():
        pltpu.sync_copy(mine_ref, root_vmem.at[0])
        pltpu.sync_copy(other_ref, root_vmem.at[1])
        pltpu.sync_copy(leaf_ref, all_keys.at[:, pl.ds(SHARED, LEAF_LEN)])
        for kind in range(2):
            all_keys[kind, 0:ROOT] = root_vmem[:, :, kind].reshape(ROOT, HD)
            all_keys[kind, ROOT:SHARED] = node_ref[:, kind].reshape(NODE_ROWS, HD)
        rows = 128
        blocks = LEAF_LEN // rows

        def some_rows(step, carry):
            start = pl.multiple_of(lax.rem(step, blocks) * rows, rows)
            place = (pl.ds(start, rows), columns_at(step // blocks, HD))
            query = q_ref[place]
            row = start + lax.broadcasted_iota(jnp.int32, (rows, NODE_ROWS), 0)
            column = lax.broadcasted_iota(jnp.int32, (rows, NODE_ROWS), 1)

            def scores_of(block):
                keys_here = all_keys[0, pl.ds(pl.multiple_of(block * NODE_ROWS, NODE_ROWS), NODE_ROWS)]
                scores = dot_t(query, keys_here) * SCORE_SCALE
                first = ROOT // NODE_ROWS
                seen = jnp.where(jnp.broadcast_to(along_ref[0:1], row.shape) > 0.5, 1, 0)
                seen = jnp.where(block < first, 1, jnp.where(block == first, seen, row >= column))
                return jnp.where(seen > 0, scores, MASKED), seen > 0

            def take_top(block, top):
                return jnp.maximum(top, jnp.max(scores_of(block)[0], 1, keepdims=True))

            top = lax.fori_loop(
                0, KEYS // NODE_ROWS, take_top, jnp.full((rows, 1), MASKED, f32)
            )

            def add_block(block, carry):
                total, attended = carry
                scores, seen = scores_of(block)
                weights = jnp.where(seen, jnp.exp(scores - top), 0.0)
                here = pl.ds(pl.multiple_of(block * NODE_ROWS, NODE_ROWS), NODE_ROWS)
                total += jnp.sum(weights, 1, keepdims=True)
                return total, attended + dot(weights.astype(bf16), all_keys[1, here])

            total, attended = lax.fori_loop(
                0,
                KEYS // NODE_ROWS,
                add_block,
                (jnp.zeros((rows, 1), f32), jnp.zeros((rows, HD), f32)),
            )
            result[place] = (attended / total).astype(bf16)
            return carry

        lax.fori_loop(0, HEADS_DEV * blocks, some_rows, 0)
        pltpu.sync_copy(result, out_ref)


vmem = pl.BlockSpec(memory_space=pltpu.VMEM)
smem = pl.BlockSpec(memory_space=pltpu.SMEM)
anywhere = pl.BlockSpec(memory_space=pl.ANY)


def limit(mib):
    return pltpu.CompilerParams(vmem_limit_bytes=mib * 2**20)


def spread(node_kv):
    return pl.pallas_call(
        spread_kernel,
        grid=(CHIPS // SPREAD,),
        in_specs=[
            pl.BlockSpec((2, NODES_DEV, SPREAD * PIECE, HD), lambda step: (0, 0, step, 0))
        ],
        out_specs=pl.BlockSpec((SPREAD, 2, NODES_DEV, PIECE, HD), lambda step: (step, 0, 0, 0, 0)),
        out_shape=pltpu.HBM((CHIPS, 2, NODES_DEV, PIECE, HD), bf16),
        compiler_params=limit(4),
        name="spread",
    )(node_kv)


def select_pieces(table, mine, other):
    return pl.pallas_call(
        select_kernel,
        in_specs=[smem, vmem, vmem],
        out_specs=vmem,
        out_shape=jax.ShapeDtypeStruct((CHIPS, 2, DEPTH, PIECE, HD), bf16),
        compiler_params=limit(8),
        name="select_pieces",
    )(table, mine, other)


sums_shape = (LEAF_LEN, HEADS_DEV * HD)
totals_shape = (LEAF_LEN, HD)


sums_out = [pltpu.HBM(sums_shape, f32), jax.ShapeDtypeStruct(totals_shape, f32)]


def attend_near(table, root, leaf_kv, queries):
    count = NEAR * TOKENS + LEAF_LEN
    return pl.pallas_call(
        near_kernel,
        in_specs=[smem] + [vmem] * 3,
        out_specs=[anywhere, vmem, vmem, vmem],
        out_shape=sums_out
        + [
            jax.ShapeDtypeStruct((NODE_ROWS, HD), f32),
            jax.ShapeDtypeStruct((8, NODE_ROWS), f32),
        ],
        scratch_shapes=[
            pltpu.VMEM((2 * HD, count), bf16),
            pltpu.VMEM((count, 2 * HD), bf16),
            pltpu.VMEM(sums_shape, f32),
            pltpu.SemaphoreType.DMA((HEADS_DEV // GROUP,)),
        ],
        compiler_params=limit(24),
        name="attend_near",
    )(table, root, leaf_kv, queries)


def attend_far(mine, other, queries, totals, sums):
    count = ROOT - NEAR * TOKENS
    return pl.pallas_call(
        far_kernel,
        in_specs=[vmem] * 4 + [anywhere],
        out_specs=[anywhere, vmem],
        out_shape=sums_out,
        input_output_aliases={4: 0},
        scratch_shapes=[
            pltpu.VMEM((2 * HD, count), bf16),
            pltpu.VMEM((count, 2 * HD), bf16),
            pltpu.VMEM(sums_shape, f32),
            pltpu.SemaphoreType.DMA((HEADS_DEV // GROUP + 1,)),
        ],
        compiler_params=limit(32),
        name="attend_far",
    )(mine, other, queries, totals, sums)


def attend_nodes(nodes, masks, totals, sums, queries, mine, other, leaf_kv):
    return pl.pallas_call(
        node_kernel,
        in_specs=[vmem] * 5 + [anywhere] * 4,
        out_specs=[anywhere] * 2,
        out_shape=[
            jax.ShapeDtypeStruct((LEAF_LEN, HEADS_DEV * HD), bf16),
            pltpu.HBM(sums_shape, f32),
        ],
        input_output_aliases={8: 1},
        scratch_shapes=[
            pltpu.VMEM((2 * HD, NODE_ROWS), bf16),
            pltpu.VMEM((NODE_ROWS, 2 * HD), bf16),
            pltpu.VMEM((CORES,) + mine.shape, bf16),
            pltpu.VMEM((2, KEYS, HD), bf16),
            pltpu.VMEM(sums_shape, f32),
            pltpu.VMEM((LEAF_LEN, HEADS_DEV * HD), bf16),
            pltpu.SemaphoreType.DMA((1 + len(NODE_GROUPS),)),
        ],
        compiler_params=limit(32),
        name="attend_nodes",
    )(
        nodes,
        *masks,
        totals,
        queries,
        mine,
        other,
        leaf_kv,
        sums,
    )[0]


def columns_of(rows, place, width):
    return lax.dynamic_slice_in_dim(rows, place * width, width, 2)


def per_device(queries, leaf_kv, root_kv, node_kv, node_len, node_slot, slot_leaf, ancestors):
    blk = lax.axis_index("blk").astype(jnp.int32).reshape(1)
    table = jnp.concatenate([slot_leaf, ancestors.T.reshape(-1), node_slot, node_len, blk])

    tp = lax.axis_index("tp").astype(jnp.int32)
    z_half, x = tp // X, tp % X
    width = X * HD
    swap = [(i, (i + X) % (2 * X)) for i in range(2 * X)]
    away = lax.ppermute(root_kv, "tp", swap)
    root = columns_of(jnp.concatenate([root_kv, away], 1), z_half, width)
    parts = [columns_of(root, x, HD)]
    for d in range(1, X):
        ring = [(h * X + i, h * X + (i + d) % X) for h in range(2) for i in range(X)]
        parts.append(lax.ppermute(columns_of(root, (x + d) % X, HD), "tp", ring))
    root = jnp.concatenate(parts, 1)[None]

    root = jnp.concatenate([root] + [lax.ppermute(root, "blk", shifted(d, 0, 0)) for d in range(1, Z)])

    pieces = spread(node_kv)
    root, pieces = lax.optimization_barrier((root, pieces))
    mine = lax.all_to_all(pieces, "blk", 0, 0, tiled=True, axis_index_groups=SAME_CORE)

    near_sums, near_totals, *masks = attend_near(table, root, leaf_kv, queries)
    root = jnp.concatenate([root] + [lax.ppermute(root, "blk", shifted(0, d, 0)) for d in range(1, Y)])
    root, mine, near_totals = lax.optimization_barrier((root, mine, near_totals))
    root_other = lax.ppermute(root, "blk", shifted(0, 0, 1))
    other = lax.ppermute(mine, "blk", shifted(0, 0, 1))
    chosen = select_pieces(table, mine, other)
    nodes = lax.all_to_all(chosen, "blk", 0, 0, tiled=True, axis_index_groups=SAME_CORE)

    sums, totals = attend_far(root, root_other, queries, near_totals, near_sums)
    return attend_nodes(nodes, masks, totals, sums, queries, root, root_other, leaf_kv)


def solution(mesh):
    placed = (
        P("blk", "tp"),
        P(None, "blk", "tp"),
        P(None, ("blk", "tp"), None),
        P(None, "blk", None, "tp"),
        P(),
        P(),
        P(),
        P(),
    )
    return jax.shard_map(
        per_device, mesh=mesh, in_specs=placed, out_specs=P("blk", "tp"), check_vma=False
    )
```

```python
import jax
import jax.numpy as jnp
from jax import lax
from jax.experimental import pallas as pl
from jax.experimental.pallas import tpu as pltpu
from jax.sharding import PartitionSpec as P

HD = 128
HEADS_DEV = 8
LEAF_LEN = 512
NODE_LEN = 256
DEPTH = 2
ROOT = 2048
X, Y, Z, CORES = 4, 4, 4, 2
CHIPS = Z * Y
PIECE = NODE_LEN // CHIPS
NODES_DEV = 4
NODE_ROWS = DEPTH * NODE_LEN
SHARED = ROOT + NODE_ROWS
KEYS = SHARED + LEAF_LEN
TOKENS = ROOT // (CHIPS * CORES)
NEAR = Z
LEAVES = 32
SLOT_LEAF, ANCESTORS, NODE_SLOT, NODE_LENS, BLK = 0, 32, 96, 224, 352
SPREAD = 8
GROUP = 4
NODE_GROUPS = ((0, 1, 2, 3, 4, 5), (6, 7))
EARLY_HEADS = 5
FAR_EARLY_HEADS = 2
SCORE_SCALE = HD**-0.5
LOG_SCALE = SCORE_SCALE * 1.4426950408889634
MASKED = -1e30
TOTAL_MIN, TOTAL_MAX = 2.0**-60, 2.0**100

bf16, f32 = jnp.bfloat16, jnp.float32


def device_at(z, y, core):
    return (z * Y + y) * CORES + core


def shifted(dz, dy, dcore):
    return [
        (device_at(z, y, c), device_at((z + dz) % Z, (y + dy) % Y, c ^ dcore))
        for z in range(Z)
        for y in range(Y)
        for c in range(CORES)
    ]


SAME_CORE = [[device_at(z, y, c) for z in range(Z) for y in range(Y)] for c in range(CORES)]


def dot(a, b):
    return jnp.dot(a, b, preferred_element_type=f32)


def dot_t(a, b):
    return lax.dot_general(a, b, (((1,), (1,)), ((), ())), preferred_element_type=f32)


def scaled_query(q):
    scaled = q.astype(f32) * LOG_SCALE
    high = scaled.astype(bf16)
    low = (scaled - high.astype(f32)).astype(bf16)
    return jnp.concatenate([high, low], 1)


def store_keys(keys_ref, first, keys):
    count = keys.shape[0]
    turned = keys.T
    keys_ref[0:HD, first : first + count] = turned
    keys_ref[HD : 2 * HD, first : first + count] = turned


def spread_kernel(node_ref, out_ref):
    for chip in range(SPREAD):
        out_ref[chip] = node_ref[:, :, chip * PIECE : (chip + 1) * PIECE]


def node_at(table_ref, blk, level):
    leaf = table_ref[SLOT_LEAF + blk]
    return table_ref[ANCESTORS + level * LEAVES + leaf]


def select_kernel(table_ref, mine_ref, other_ref, out_ref):
    core = lax.rem(table_ref[BLK], CORES)
    for chip in range(CHIPS):
        for level in range(DEPTH):
            slot = table_ref[NODE_SLOT + node_at(table_ref, chip * CORES + core, level)]
            owner = slot // NODES_DEV
            place = lax.rem(slot, NODES_DEV)
            source = owner // CORES
            out_ref[chip, :, level] = jnp.where(
                lax.rem(owner, CORES) == core,
                mine_ref[source, :, place],
                other_ref[source, :, place],
            )


def store_values(values_ref, first, rows):
    count = rows.shape[0]
    values_ref[first : first + count, 0:HD] = rows
    values_ref[first : first + count, HD : 2 * HD] = jnp.ones((count, HD), bf16)


def weigh(query, keys, values, shown=None):
    scores = dot(query, keys)
    if shown is not None:
        scores = jnp.where(shown, scores, MASKED)
    return dot(jnp.exp2(scores).astype(bf16), values)


def columns_at(step, width):
    return pl.ds(pl.multiple_of(step * width, width), width)


def total_column(head):
    return head * (HD // HEADS_DEV)


def store_total(totals_ref, head, total):
    if head:
        lane = lax.broadcasted_iota(jnp.int32, (LEAF_LEN, HD), 1)
        total = jnp.where(lane >= total_column(head), total, totals_ref[...])
    totals_ref[...] = total


def store_group(copies, sums, sums_hbm, sems, head):
    if (head + 1) % GROUP == 0:
        part = slice((head + 1 - GROUP) * HD, (head + 1) * HD)
        copy = pltpu.make_async_copy(
            sums.at[:, part], sums_hbm.at[:, part], sems.at[head // GROUP]
        )
        copy.start()
        copies.append(copy)


def store_root(keys, values, first, parts):
    count = parts.shape[0] * parts.shape[2]
    store_keys(keys, first, parts[:, 0].reshape(count, HD))
    store_values(values, first, parts[:, 1].reshape(count, HD))


def near_kernel(
    table_ref,
    root_ref,
    leaf_ref,
    q_ref,
    sums_hbm,
    totals_ref,
    down_ref,
    along_ref,
    keys,
    values,
    sums,
    sems,
):
    blk = table_ref[BLK]
    first_len = table_ref[NODE_LENS + node_at(table_ref, blk, 0)]
    second_len = table_ref[NODE_LENS + node_at(table_ref, blk, 1)]
    for ref, dim in ((down_ref, 0), (along_ref, 1)):
        r = lax.broadcasted_iota(jnp.int32, ref.shape, dim)
        token = (r >> 5) * PIECE + (r & (PIECE - 1))
        length = jnp.where((r & PIECE) == 0, first_len, second_len)
        ref[...] = jnp.where(token < length, 1.0, 0.0)
    near = NEAR * TOKENS
    store_root(keys, values, 0, root_ref)
    store_keys(keys, near, leaf_ref[0])
    store_values(values, near, leaf_ref[1])
    half = LEAF_LEN // 2
    middle, last = near + half, near + LEAF_LEN
    row = lax.broadcasted_iota(jnp.int32, (half, half), 0)
    column = lax.broadcasted_iota(jnp.int32, (half, half), 1)
    causal = row >= column
    copies = []
    for head in range(HEADS_DEV):
        columns = slice(head * HD, (head + 1) * HD)
        query = scaled_query(q_ref[:, columns])
        upper, lower = query[:half], query[half:]
        acc_upper = weigh(upper, keys[:, :near], values[:near]) + weigh(
            upper, keys[:, near:middle], values[near:middle], causal
        )
        acc_lower = weigh(lower, keys[:, :middle], values[:middle]) + weigh(
            lower, keys[:, middle:last], values[middle:last], causal
        )
        sums[:half, columns] = acc_upper[:, :HD]
        sums[half:, columns] = acc_lower[:, :HD]
        store_total(totals_ref, head, jnp.concatenate([acc_upper[:, HD:], acc_lower[:, HD:]]))
        store_group(copies, sums, sums_hbm, sems, head)
    for copy in copies:
        copy.wait()


def far_kernel(
    mine_ref,
    other_ref,
    q_ref,
    near_totals_ref,
    near_sums_hbm,
    sums_hbm,
    totals_ref,
    keys,
    values,
    sums,
    sems,
):
    arrival = pltpu.make_async_copy(near_sums_hbm, sums, sems.at[HEADS_DEV // GROUP])
    arrival.start()
    store_root(keys, values, 0, mine_ref[NEAR:])
    store_root(keys, values, (CHIPS - NEAR) * TOKENS, other_ref)
    copies = []
    held = []
    for head in range(HEADS_DEV):
        columns = slice(head * HD, (head + 1) * HD)
        held.append((head, weigh(scaled_query(q_ref[:, columns]), keys[...], values[...])))
        if head + 1 < FAR_EARLY_HEADS:
            continue
        if head + 1 == FAR_EARLY_HEADS:
            arrival.wait()
        for place, acc in held:
            columns = slice(place * HD, (place + 1) * HD)
            sums[:, columns] += acc[:, :HD]
            store_total(totals_ref, place, acc[:, HD:])
            store_group(copies, sums, sums_hbm, sems, place)
        held = []
    totals_ref[...] += near_totals_ref[...]
    for copy in copies:
        copy.wait()


def node_kernel(
    node_ref,
    down_ref,
    along_ref,
    totals_ref,
    q_ref,
    mine_ref,
    other_ref,
    leaf_ref,
    sums_hbm,
    out_ref,
    _,
    keys,
    values,
    root_vmem,
    all_keys,
    earlier_sums,
    result,
    sems,
):
    arrival = pltpu.make_async_copy(sums_hbm, earlier_sums, sems.at[0])
    arrival.start()
    shown = down_ref[...] > 0.5
    node_keys = node_ref[:, 0].reshape(NODE_ROWS, HD).astype(f32)
    node_values = node_ref[:, 1].reshape(NODE_ROWS, HD).astype(f32)
    store_keys(keys, 0, jnp.where(shown, node_keys, 0.0).astype(bf16))
    values[:, 0:HD] = jnp.where(shown, node_values, 0.0).astype(bf16)
    values[:, HD : 2 * HD] = down_ref[...].astype(bf16)

    outside = jnp.zeros((LEAF_LEN, HD), f32)
    copies = []
    held = []
    for heads in NODE_GROUPS:
        for head in heads:
            columns = slice(head * HD, (head + 1) * HD)
            held.append((head, weigh(scaled_query(q_ref[:, columns]), keys[...], values[...])))
            if head + 1 < EARLY_HEADS:
                continue
            if head + 1 == EARLY_HEADS:
                arrival.wait()
            for place, acc in held:
                columns = slice(place * HD, (place + 1) * HD)
                first = total_column(place)
                total = acc[:, HD:] + totals_ref[:, first : first + 1]
                outside = jnp.where((total >= TOTAL_MIN) & (total <= TOTAL_MAX), outside, 1.0)
                sums = acc[:, :HD] + earlier_sums[:, columns]
                result[:, columns] = (sums / total).astype(bf16)
            held = []
        part = slice(heads[0] * HD, (heads[-1] + 1) * HD)
        copy = pltpu.make_async_copy(
            result.at[:, part], out_ref.at[:, part], sems.at[1 + len(copies)]
        )
        copy.start()
        copies.append(copy)
    for copy in copies:
        copy.wait()

    @pl.when(jnp.max(outside) > 0.5)
    def _():
        pltpu.sync_copy(mine_ref, root_vmem.at[0])
        pltpu.sync_copy(other_ref, root_vmem.at[1])
        pltpu.sync_copy(leaf_ref, all_keys.at[:, pl.ds(SHARED, LEAF_LEN)])
        for kind in range(2):
            all_keys[kind, 0:ROOT] = root_vmem[:, :, kind].reshape(ROOT, HD)
            all_keys[kind, ROOT:SHARED] = node_ref[:, kind].reshape(NODE_ROWS, HD)
        rows = 128
        blocks = LEAF_LEN // rows

        def some_rows(step, carry):
            start = pl.multiple_of(lax.rem(step, blocks) * rows, rows)
            place = (pl.ds(start, rows), columns_at(step // blocks, HD))
            query = q_ref[place]
            row = start + lax.broadcasted_iota(jnp.int32, (rows, NODE_ROWS), 0)
            column = lax.broadcasted_iota(jnp.int32, (rows, NODE_ROWS), 1)

            def scores_of(block):
                keys_here = all_keys[0, pl.ds(pl.multiple_of(block * NODE_ROWS, NODE_ROWS), NODE_ROWS)]
                scores = dot_t(query, keys_here) * SCORE_SCALE
                first = ROOT // NODE_ROWS
                seen = jnp.where(jnp.broadcast_to(along_ref[0:1], row.shape) > 0.5, 1, 0)
                seen = jnp.where(block < first, 1, jnp.where(block == first, seen, row >= column))
                return jnp.where(seen > 0, scores, MASKED), seen > 0

            def take_top(block, top):
                return jnp.maximum(top, jnp.max(scores_of(block)[0], 1, keepdims=True))

            top = lax.fori_loop(
                0, KEYS // NODE_ROWS, take_top, jnp.full((rows, 1), MASKED, f32)
            )

            def add_block(block, carry):
                total, attended = carry
                scores, seen = scores_of(block)
                weights = jnp.where(seen, jnp.exp(scores - top), 0.0)
                here = pl.ds(pl.multiple_of(block * NODE_ROWS, NODE_ROWS), NODE_ROWS)
                total += jnp.sum(weights, 1, keepdims=True)
                return total, attended + dot(weights.astype(bf16), all_keys[1, here])

            total, attended = lax.fori_loop(
                0,
                KEYS // NODE_ROWS,
                add_block,
                (jnp.zeros((rows, 1), f32), jnp.zeros((rows, HD), f32)),
            )
            result[place] = (attended / total).astype(bf16)
            return carry

        lax.fori_loop(0, HEADS_DEV * blocks, some_rows, 0)
        pltpu.sync_copy(result, out_ref)


vmem = pl.BlockSpec(memory_space=pltpu.VMEM)
smem = pl.BlockSpec(memory_space=pltpu.SMEM)
anywhere = pl.BlockSpec(memory_space=pl.ANY)


def limit(mib):
    return pltpu.CompilerParams(vmem_limit_bytes=mib * 2**20)


def spread(node_kv):
    return pl.pallas_call(
        spread_kernel,
        grid=(CHIPS // SPREAD,),
        in_specs=[
            pl.BlockSpec((2, NODES_DEV, SPREAD * PIECE, HD), lambda step: (0, 0, step, 0))
        ],
        out_specs=pl.BlockSpec((SPREAD, 2, NODES_DEV, PIECE, HD), lambda step: (step, 0, 0, 0, 0)),
        out_shape=pltpu.HBM((CHIPS, 2, NODES_DEV, PIECE, HD), bf16),
        compiler_params=limit(4),
        name="spread",
    )(node_kv)


def select_pieces(table, mine, other):
    return pl.pallas_call(
        select_kernel,
        in_specs=[smem, vmem, vmem],
        out_specs=vmem,
        out_shape=jax.ShapeDtypeStruct((CHIPS, 2, DEPTH, PIECE, HD), bf16),
        compiler_params=limit(8),
        name="select_pieces",
    )(table, mine, other)


sums_shape = (LEAF_LEN, HEADS_DEV * HD)
totals_shape = (LEAF_LEN, HD)


sums_out = [pltpu.HBM(sums_shape, f32), jax.ShapeDtypeStruct(totals_shape, f32)]


def attend_near(table, root, leaf_kv, queries):
    count = NEAR * TOKENS + LEAF_LEN
    return pl.pallas_call(
        near_kernel,
        in_specs=[smem] + [vmem] * 3,
        out_specs=[anywhere, vmem, vmem, vmem],
        out_shape=sums_out
        + [
            jax.ShapeDtypeStruct((NODE_ROWS, HD), f32),
            jax.ShapeDtypeStruct((8, NODE_ROWS), f32),
        ],
        scratch_shapes=[
            pltpu.VMEM((2 * HD, count), bf16),
            pltpu.VMEM((count, 2 * HD), bf16),
            pltpu.VMEM(sums_shape, f32),
            pltpu.SemaphoreType.DMA((HEADS_DEV // GROUP,)),
        ],
        compiler_params=limit(24),
        name="attend_near",
    )(table, root, leaf_kv, queries)


def attend_far(mine, other, queries, totals, sums):
    count = ROOT - NEAR * TOKENS
    return pl.pallas_call(
        far_kernel,
        in_specs=[vmem] * 4 + [anywhere],
        out_specs=[anywhere, vmem],
        out_shape=sums_out,
        input_output_aliases={4: 0},
        scratch_shapes=[
            pltpu.VMEM((2 * HD, count), bf16),
            pltpu.VMEM((count, 2 * HD), bf16),
            pltpu.VMEM(sums_shape, f32),
            pltpu.SemaphoreType.DMA((HEADS_DEV // GROUP + 1,)),
        ],
        compiler_params=limit(32),
        name="attend_far",
    )(mine, other, queries, totals, sums)


def attend_nodes(nodes, masks, totals, sums, queries, mine, other, leaf_kv):
    return pl.pallas_call(
        node_kernel,
        in_specs=[vmem] * 5 + [anywhere] * 4,
        out_specs=[anywhere] * 2,
        out_shape=[
            jax.ShapeDtypeStruct((LEAF_LEN, HEADS_DEV * HD), bf16),
            pltpu.HBM(sums_shape, f32),
        ],
        input_output_aliases={8: 1},
        scratch_shapes=[
            pltpu.VMEM((2 * HD, NODE_ROWS), bf16),
            pltpu.VMEM((NODE_ROWS, 2 * HD), bf16),
            pltpu.VMEM((CORES,) + mine.shape, bf16),
            pltpu.VMEM((2, KEYS, HD), bf16),
            pltpu.VMEM(sums_shape, f32),
            pltpu.VMEM((LEAF_LEN, HEADS_DEV * HD), bf16),
            pltpu.SemaphoreType.DMA((1 + len(NODE_GROUPS),)),
        ],
        compiler_params=limit(32),
        name="attend_nodes",
    )(
        nodes,
        *masks,
        totals,
        queries,
        mine,
        other,
        leaf_kv,
        sums,
    )[0]


def columns_of(rows, place, width):
    return lax.dynamic_slice_in_dim(rows, place * width, width, 2)


def per_device(queries, leaf_kv, root_kv, node_kv, node_len, node_slot, slot_leaf, ancestors):
    blk = lax.axis_index("blk").astype(jnp.int32).reshape(1)
    table = jnp.concatenate([slot_leaf, ancestors.T.reshape(-1), node_slot, node_len, blk])

    tp = lax.axis_index("tp").astype(jnp.int32)
    z_half, x = tp // X, tp % X
    width = X * HD
    swap = [(i, (i + X) % (2 * X)) for i in range(2 * X)]
    away = lax.ppermute(root_kv, "tp", swap)
    root = columns_of(jnp.concatenate([root_kv, away], 1), z_half, width)
    parts = [columns_of(root, x, HD)]
    for d in range(1, X):
        ring = [(h * X + i, h * X + (i + d) % X) for h in range(2) for i in range(X)]
        parts.append(lax.ppermute(columns_of(root, (x + d) % X, HD), "tp", ring))
    root = jnp.concatenate(parts, 1)[None]

    root = jnp.concatenate([root] + [lax.ppermute(root, "blk", shifted(d, 0, 0)) for d in range(1, Z)])

    pieces = spread(node_kv)
    root, pieces = lax.optimization_barrier((root, pieces))
    mine = lax.all_to_all(pieces, "blk", 0, 0, tiled=True, axis_index_groups=SAME_CORE)

    near_sums, near_totals, *masks = attend_near(table, root, leaf_kv, queries)
    root = jnp.concatenate([root] + [lax.ppermute(root, "blk", shifted(0, d, 0)) for d in range(1, Y)])
    root, mine, near_totals = lax.optimization_barrier((root, mine, near_totals))
    root_other = lax.ppermute(root, "blk", shifted(0, 0, 1))
    other = lax.ppermute(mine, "blk", shifted(0, 0, 1))
    chosen = select_pieces(table, mine, other)
    nodes = lax.all_to_all(chosen, "blk", 0, 0, tiled=True, axis_index_groups=SAME_CORE)

    sums, totals = attend_far(root, root_other, queries, near_totals, near_sums)
    return attend_nodes(nodes, masks, totals, sums, queries, root, root_other, leaf_kv)


def solution(mesh):
    placed = (
        P("blk", "tp"),
        P(None, "blk", "tp"),
        P(None, ("blk", "tp"), None),
        P(None, "blk", None, "tp"),
        P(),
        P(),
        P(),
        P(),
    )
    return jax.shard_map(
        per_device, mesh=mesh, in_specs=placed, out_specs=P("blk", "tp"), check_vma=False
    )
```
